32 devices in a mesh: groups: 2 (over x), ctx: 8 (over z, y), head: 2 (over core).
Axes of the slice: x: 2, y: 2, z: 4, core: 2. Of those that a mesh axis runs over, the one named last changes fastest.
Arguments:
- query_rows: bfloat16 [4096, 2048], P(('groups', 'ctx'), 'head'), parts along dimension 0, may hold values from -6 to 6
- key_rows: bfloat16 [4096, 256], P(('groups', 'ctx'), 'head'), parts along dimension 0, may hold values from -6 to 6
- value_rows: bfloat16 [4096, 256], P(('groups', 'ctx'), 'head'), parts along dimension 0, may hold values from -6 to 6
- out_grad: bfloat16 [4096, 2048], P(('groups', 'ctx'), 'head'), parts along dimension 0, may hold values from -6 to 6
- doc_lengths: int32 [32], P('groups'), parts along dimension 0, may hold values from 1 to 256, 2048 in all
Outputs:
- attended: bfloat16 [4096, 2048], P(('groups', 'ctx'), 'head'), parts along dimension 0
- query_grad: bfloat16 [4096, 2048], P(('groups', 'ctx'), 'head'), parts along dimension 0
- key_grad: bfloat16 [4096, 256], P(('groups', 'ctx'), 'head'), parts along dimension 0
- value_grad: bfloat16 [4096, 256], P(('groups', 'ctx'), 'head'), parts along dimension 0
The draws below stay inside these ranges and needn't reach their ends.
There are 2 independent parts, one for each index of `groups`. The reference program is written for one: setup_inputs(seed, part) draws one part's arguments, and reference() takes and returns one part's arrays. A program takes and returns all parts, laid end to end along the dimension named above; each array names one. Nothing has to cross between parts.
Inputs may be any that keep to these rules, and one draw needn't show every extreme that they name: `doc_lengths`: documents are laid end to end in position order and their lengths sum to 2048; the longest has exactly 256 tokens.
All inputs are finite; a program needn't handle non-finite values.
Results may differ from the reference program's by a relative error of at most 0.017.
Values may be sent and summed in bfloat16 or wider, within the bound.
A program may use at most 64 MiB of HBM per device.

```python
import math
import jax
import jax.numpy as jnp
import numpy as np
from jax import lax

HEADS = 16
KV_HEADS = 2
HEAD_DIM = 128
TOK_DEV = 256
STRETCH = 128
TOKENS = 2048
DOCMAX = 256
NDOCS = 16
N_CTX = 8


def rough_entries(key, row_total, col_total):
    entries = jax.random.normal(jax.random.fold_in(key, 1), (row_total, col_total), jnp.float32)
    return jnp.clip(entries, -6.0, 6.0)


def draw_query_rows(key, part):
    own_key = jax.random.fold_in(key, 101)
    entries = rough_entries(own_key, TOKENS, HEADS * HEAD_DIM)
    return entries.astype(jnp.bfloat16)


def draw_key_rows(key, part):
    own_key = jax.random.fold_in(key, 202)
    entries = rough_entries(own_key, TOKENS, KV_HEADS * HEAD_DIM)
    return entries.astype(jnp.bfloat16)


def block_scale(stream_key, extent, split, least, high):
    gain = 1.0
    for dim, parts in split:
        draws = jax.random.uniform(jax.random.fold_in(jax.random.fold_in(stream_key, 6), dim), (parts,), jnp.float32, least / len(split), high / len(split))
        gain = gain * jnp.repeat(jnp.exp(draws), extent[dim] // parts).reshape((-1,) + (1,) * (len(extent) - 1 - dim))
    return gain


def length_profile(amount, total, reach, skew):
    loads = [(1 << 20) // math.isqrt(rank ** skew) + 1 for rank in range(2, amount + 1)]
    surplus, counts = total - reach - (amount - 1), [1] * (amount - 1)
    while surplus > 0:
        free = [i for i in range(amount - 1) if counts[i] < reach]
        whole, remaining = sum([loads[i] for i in free]), surplus
        for i in free:
            extra = min(reach - counts[i], max(1, remaining * loads[i] // whole), surplus)
            counts[i] = counts[i] + extra
            surplus = surplus - extra
    return np.array([reach] + counts)


def ragged(rng, number_of, total, most, skew):
    if number_of == 2:
        one = jax.random.randint(rng, (), max(1, total - most), min(most, total - 1) + 1)
        return jnp.stack([one, total - one])
    tallies = jnp.asarray(length_profile(number_of, total, most, skew), jnp.int32)
    couples = (number_of - 1) // 2
    donor, sink = tallies[1:1 + 2 * couples:2], tallies[2:2 + 2 * couples:2]
    slack = jnp.minimum(donor - 1, most - sink)
    passed = jax.random.randint(jax.random.fold_in(rng, 1), (couples,), 0, 1 << 20) % (slack + 1)
    tallies = tallies.at[1:1 + 2 * couples:2].set(donor - passed).at[2:2 + 2 * couples:2].set(sink + passed)
    return tallies[jax.random.permutation(jax.random.fold_in(rng, 2), number_of)]


def centred(key, shape, deviation, most, pieces=(), kind=jnp.bfloat16):
    values = jax.random.normal(key, shape, jnp.float32) * deviation
    if len(pieces) > 0:
        values = block_scale(key, shape, pieces, -0.22, 0.18) * values
    return jnp.clip(values, min=-most, max=most).astype(kind)


def setup_inputs(seed: int = 0, part: int = 0) -> dict:
    key_list = jax.random.split(jax.random.key(seed), 6)
    part_splits = jax.random.split(jax.random.fold_in(key_list[5], part), 6)
    query_rows = draw_query_rows(jax.random.fold_in(jax.random.fold_in(key_list[5], part), 71), part)
    key_rows = draw_key_rows(jax.random.fold_in(jax.random.fold_in(key_list[5], part), 71), part)
    value_rows = centred(part_splits[2], (TOKENS, KV_HEADS * HEAD_DIM), 1.0, 6.0, ((0, 8), (1, 2)))
    out_grad = centred(part_splits[3], (TOKENS, HEADS * HEAD_DIM), 1.0, 6.0, ((0, 8), (1, 2)))
    doc_lengths = ragged(part_splits[4], NDOCS, TOKENS, DOCMAX, 2).astype(jnp.int32)
    return dict(query_rows=query_rows, key_rows=key_rows, value_rows=value_rows, out_grad=out_grad, doc_lengths=doc_lengths)


def row_positions(row_total, stretch_len, ctx_count):
    row_index = jnp.arange(row_total, dtype=jnp.int32)
    device = row_index // (2 * stretch_len)
    upper_half = (row_index // stretch_len) % 2
    stretch_id = jnp.where(upper_half == 0, device, 2 * ctx_count - 1 - device)
    return (stretch_id * stretch_len + row_index % stretch_len).astype(jnp.int32)


def position_rows(row_total, stretch_len, ctx_count):
    position = jnp.arange(row_total, dtype=jnp.int32)
    stretch_id = position // stretch_len
    device = jnp.where(stretch_id < ctx_count, stretch_id, 2 * ctx_count - 1 - stretch_id)
    upper_half = jnp.where(stretch_id < ctx_count, 0, 1)
    return (device * 2 * stretch_len + upper_half * stretch_len + position % stretch_len).astype(jnp.int32)


def documents(positions, doc_lengths):
    starts = jnp.cumsum(doc_lengths) - doc_lengths
    return (jnp.sum((starts[None, :] <= positions[:, None]).astype(jnp.int32), axis=1) - 1).astype(jnp.int32)


def settle(entries):
    return lax.optimization_barrier(entries.astype(jnp.bfloat16)).astype(jnp.float32)


def reference(query_rows, key_rows, value_rows, out_grad, doc_lengths):
    group_size = HEADS // KV_HEADS
    scaling = HEAD_DIM ** -0.5
    block_len = TOK_DEV
    span_len = DOCMAX + block_len
    order = position_rows(TOKENS, STRETCH, N_CTX)
    inverse = row_positions(TOKENS, STRETCH, N_CTX)
    queries = query_rows[order].reshape(TOKENS, KV_HEADS, group_size, HEAD_DIM)
    grads = out_grad[order].reshape(TOKENS, KV_HEADS, group_size, HEAD_DIM)
    pad_rows = jnp.zeros((DOCMAX, KV_HEADS, HEAD_DIM), key_rows.dtype)
    key_pad = jnp.concatenate([pad_rows, key_rows[order].reshape(TOKENS, KV_HEADS, HEAD_DIM)], axis=0)
    value_pad = jnp.concatenate([pad_rows, value_rows[order].reshape(TOKENS, KV_HEADS, HEAD_DIM)], axis=0)
    positions = jnp.arange(TOKENS, dtype=jnp.int32)
    doc_ids = documents(positions, doc_lengths)
    key_pos = jnp.concatenate([jnp.zeros((DOCMAX,), jnp.int32), positions])
    key_doc = jnp.concatenate([jnp.full((DOCMAX,), -1, dtype=jnp.int32), doc_ids])

    def block(carried, block_index):
        key_full, value_full = carried
        row_start = (block_index * block_len).astype(jnp.int32)
        query_block = lax.dynamic_slice_in_dim(queries, row_start, block_len, 0).astype(jnp.float32)
        grad_block = lax.dynamic_slice_in_dim(grads, row_start, block_len, 0).astype(jnp.float32)
        query_pos = lax.dynamic_slice_in_dim(positions, row_start, block_len, 0)
        query_doc = lax.dynamic_slice_in_dim(doc_ids, row_start, block_len, 0)
        key_block = lax.dynamic_slice_in_dim(key_pad, row_start, span_len, 0).astype(jnp.float32)
        value_block = lax.dynamic_slice_in_dim(value_pad, row_start, span_len, 0).astype(jnp.float32)
        span_pos = lax.dynamic_slice_in_dim(key_pos, row_start, span_len, 0)
        span_doc = lax.dynamic_slice_in_dim(key_doc, row_start, span_len, 0)
        allowed = (span_doc[None, :] == query_doc[:, None]) & (span_pos[None, :] <= query_pos[:, None])
        allowed = allowed[:, None, None, :]
        scores = jnp.einsum("qgjd,kgd->qgjk", query_block, key_block) * scaling
        masked = jnp.where(allowed, scores, -jnp.inf)
        row_top = jnp.max(masked, axis=-1)
        log_total = row_top + jnp.log(jnp.sum(jnp.exp(masked - row_top[..., None]), axis=-1))
        weights = jnp.exp(jnp.where(allowed, scores - log_total[..., None], -jnp.inf))
        weights_low = settle(weights)
        attended_block = jnp.einsum("qgjk,kgd->qgjd", weights_low, value_block).astype(jnp.bfloat16)
        row_delta = jnp.sum(grad_block * attended_block.astype(jnp.float32), axis=-1)
        weight_grad = jnp.einsum("qgjd,kgd->qgjk", grad_block, value_block)
        score_grad = settle(weights * (weight_grad - row_delta[..., None]))
        query_block_grad = (jnp.einsum("qgjk,kgd->qgjd", score_grad, key_block) * scaling).astype(jnp.bfloat16)
        key_part = jnp.einsum("qgjk,qgjd->kgd", score_grad, query_block) * scaling
        value_part = jnp.einsum("qgjk,qgjd->kgd", weights_low, grad_block)
        previous = lax.dynamic_slice_in_dim(key_full, row_start, span_len, 0)
        key_full = lax.dynamic_update_slice_in_dim(key_full, previous + key_part, row_start, 0)
        previous = lax.dynamic_slice_in_dim(value_full, row_start, span_len, 0)
        value_full = lax.dynamic_update_slice_in_dim(value_full, previous + value_part, row_start, 0)
        return (key_full, value_full), (attended_block, query_block_grad)

    start_state = (jnp.zeros((DOCMAX + TOKENS, KV_HEADS, HEAD_DIM), jnp.float32),
                   jnp.zeros((DOCMAX + TOKENS, KV_HEADS, HEAD_DIM), jnp.float32))
    (key_full, value_full), (attended_pos, query_pos_grad) = lax.scan(
        block, start_state, jnp.arange(TOKENS // block_len, dtype=jnp.int32))
    attended = attended_pos.reshape(TOKENS, HEADS * HEAD_DIM)[inverse]
    query_grad = query_pos_grad.reshape(TOKENS, HEADS * HEAD_DIM)[inverse]
    key_grad = key_full[DOCMAX:].reshape(TOKENS, KV_HEADS * HEAD_DIM)[inverse].astype(jnp.bfloat16)
    value_grad = value_full[DOCMAX:].reshape(TOKENS, KV_HEADS * HEAD_DIM)[inverse].astype(jnp.bfloat16)
    return (attended, query_grad, key_grad, value_grad)
```

```python
import functools
import math

import jax
import jax.numpy as jnp
from jax import lax
from jax.experimental import pallas as pl
from jax.experimental.pallas import tpu as pltpu
from jax.sharding import PartitionSpec as P

HEAD_DIM = 128
DOC_STRETCHES = 8
PAIR = 2
MESH = pl.DeviceIdType.MESH
NT = (((1,), (1,)), ((), ()))


def kernel(
    n,
    reach,
    heads,
    docs_ref,
    q_hbm,
    k_hbm,
    v_hbm,
    g_hbm,
    att_ref,
    dq_ref,
    dk_ref,
    dv_ref,
    q_buf,
    g_buf,
    k_buf,
    v_buf,
    s_own,
    w_own,
    p_buf,
    d_buf,
    part_out,
    part_in,
    load_sem,
    kv_send,
    kv_recv,
    part_send,
    part_recv,
):
    st = q_hbm.shape[0] // 2
    me = lax.axis_index("ctx")
    last = 2 * n - 1
    scaling = HEAD_DIM**-0.5
    wide = PAIR * HEAD_DIM
    rows = [slice(half * st, (half + 1) * st) for half in range(2)]
    dot = functools.partial(lax.dot_general, preferred_element_type=jnp.float32)

    def matmul(a, b):
        return dot(a, b, (((1,), (0,)), ((), ())))

    loads = []
    for half in range(2):
        for slot, (src, dst) in enumerate(
            (
                (k_hbm, k_buf.at[half, 0]),
                (q_hbm, q_buf.at[half]),
                (v_hbm, v_buf.at[half, 0]),
                (g_hbm, g_buf.at[half]),
            )
        ):
            copy = pltpu.make_async_copy(src.at[rows[half]], dst, load_sem.at[half, slot])
            copy.start()
            loads.append(copy)

    barrier = pltpu.get_barrier_semaphore()
    for by in range(1, reach + 1):
        for sign in (-1, 1):
            other = me + sign * by

            @pl.when((other >= 0) & (other < n))
            def _():
                pl.semaphore_signal(
                    barrier, inc=1, device_id={"ctx": other}, device_id_type=MESH
                )

    for d in range(1, reach + 1):

        @pl.when(me < d)
        def _():
            k_buf[0, d] = jnp.zeros_like(k_buf[0, d])
            v_buf[0, d] = jnp.zeros_like(v_buf[0, d])
            part_in[1, d - 1] = jnp.zeros_like(part_in[1, d - 1])

    pl.semaphore_wait(barrier, jnp.minimum(me, reach) + jnp.minimum(n - 1 - me, reach))

    def kv_copies(half, d, target, to_half):
        return [
            pltpu.make_async_remote_copy(
                src_ref=src.at[rows[half]],
                dst_ref=dst.at[to_half, d],
                send_sem=kv_send.at[half, d - 1, which],
                recv_sem=kv_recv.at[to_half, d - 1, which],
                device_id={"ctx": target},
                device_id_type=MESH,
            )
            for which, (src, dst) in enumerate(((k_hbm, k_buf), (v_hbm, v_buf)))
        ]

    def kv_routes(act):
        for d in range(1, reach + 1):
            up = me + d
            fold = last - up

            @pl.when(up < n)
            def _():
                for copy in kv_copies(0, d, up, 0):
                    act(copy)

            @pl.when((up >= n) & (fold != me))
            def _():
                for copy in kv_copies(0, d, fold, 1):
                    act(copy)

            @pl.when(me >= d)
            def _():
                for copy in kv_copies(1, d, me - d, 1):
                    act(copy)

    kv_routes(lambda copy: copy.start())

    lane = lax.broadcasted_iota(jnp.int32, (st, st), 1)
    sub = lax.broadcasted_iota(jnp.int32, (st, st), 0)
    lower = sub <= lane
    lower_low = lower.astype(jnp.float32).astype(jnp.bfloat16)
    lower_wide = jnp.concatenate([lower] * PAIR, axis=1)
    lower_low = jnp.concatenate([lower_low] * PAIR, axis=1)
    bias = []
    for half in range(2):
        stretch = me if half == 0 else last - me
        base = stretch * st
        row_pos = base + lane[:8]
        first = jnp.zeros((8, st), jnp.int32)
        begin = jnp.int32(0)
        for i in range(docs_ref.shape[0]):
            first = jnp.where(row_pos >= begin, begin, first)
            begin = begin + docs_ref[i]
        first = first[:1] - base
        blocks = [jnp.where(lower, sub, sub - reach * st)]
        blocks += [sub - d * st for d in range(1, reach)]
        blocks = [jnp.where(block >= first, 0.0, -1e30) for block in blocks]
        bias.append([jnp.concatenate([block] * PAIR, axis=1) for block in blocks])

    def gather(buf, half, first, count):
        cols = [
            buf[half, :, h * HEAD_DIM : (h + 1) * HEAD_DIM] for h in range(first, first + count)
        ]
        return jnp.concatenate(cols, axis=0)

    for copy in loads:
        copy.wait()

    for d in range(1, reach + 1):

        @pl.when(last - me - d == me)
        def _():
            k_buf[1, d] = k_buf[0, 0]
            v_buf[1, d] = v_buf[0, 0]

    for half in range(2):
        for h in range(0, heads, PAIR):
            cols = slice(h * HEAD_DIM, h * HEAD_DIM + wide)
            s_own[half, :, cols] = dot(k_buf[half, 0], gather(q_buf, half, h, PAIR), NT)
            w_own[half, :, cols] = dot(v_buf[half, 0], gather(g_buf, half, h, PAIR), NT)

    def part_copy(half, d, target, to_half):
        return pltpu.make_async_remote_copy(
            src_ref=part_out.at[half, d - 1],
            dst_ref=part_in.at[to_half, d - 1],
            send_sem=part_send.at[half, d - 1],
            recv_sem=part_recv.at[to_half, d - 1],
            device_id={"ctx": target},
            device_id_type=MESH,
        )

    def part_routes(half, d, act):
        if half == 0:

            @pl.when(me >= d)
            def _():
                act(part_copy(0, d, me - d, 0))

        else:
            up = me + d
            fold = last - up

            @pl.when(up < n)
            def _():
                act(part_copy(1, d, up, 1))

            @pl.when((up >= n) & (fold != me))
            def _():
                act(part_copy(1, d, fold, 0))

    def wait_kv(half, d):
        for copy in kv_copies(half, d, me, half):
            copy.wait_recv()

    for half in range(2):
        for d in range(1, reach + 1):
            arrives = (me >= d) if half == 0 else (last - me - d != me)

            @pl.when(arrives)
            def _():
                wait_kv(half, d)

        for h in range(0, heads, PAIR):
            cols = slice(h * HEAD_DIM, h * HEAD_DIM + wide)
            q_cols = gather(q_buf, half, h, PAIR)
            g_cols = gather(g_buf, half, h, PAIR)
            far = dot(k_buf[half, reach], q_cols, NT)
            scores = [jnp.where(lower_wide, s_own[half, :, cols], far)]
            scores += [dot(k_buf[half, d], q_cols, NT) for d in range(1, reach)]
            scores = [score + mask for score, mask in zip(scores, bias[half])]
            top = functools.reduce(jnp.maximum, scores)
            top = jnp.max(top, axis=0, keepdims=True)
            factor = scaling * math.log2(math.e)
            weights = [jnp.exp2((score - top) * factor) for score in scores]
            total = jnp.sum(functools.reduce(jnp.add, weights), axis=0, keepdims=True)
            inverse = 1.0 / total
            weights = [weight * inverse for weight in weights]
            far = dot(v_buf[half, reach], g_cols, NT)
            grads = [jnp.where(lower_wide, w_own[half, :, cols], far)]
            grads += [dot(v_buf[half, d], g_cols, NT) for d in range(1, reach)]
            delta = functools.reduce(jnp.add, [w * g for w, g in zip(weights, grads)])
            delta = jnp.sum(delta, axis=0, keepdims=True)
            for d in range(reach):
                low = weights[d].astype(jnp.bfloat16)
                slope = (weights[d] * (grads[d] - delta)).astype(jnp.bfloat16)
                if d == 0:
                    low_own = low * lower_low
                    slope_own = slope * lower_low
                    p_buf[half, :st, cols] = low_own
                    d_buf[half, :st, cols] = slope_own
                    p_buf[half, reach * st :, cols] = low - low_own
                    d_buf[half, reach * st :, cols] = slope - slope_own
                else:
                    p_buf[half, d * st : (d + 1) * st, cols] = low
                    d_buf[half, d * st : (d + 1) * st, cols] = slope

        part_out[half, :, :st] = (
            (matmul(d_buf[half, st:], gather(q_buf, half, 0, heads)) * scaling)
            .astype(jnp.bfloat16)
            .reshape(reach, st, HEAD_DIM)
        )
        part_out[half, :, st:] = (
            matmul(p_buf[half, st:], gather(g_buf, half, 0, heads))
            .astype(jnp.bfloat16)
            .reshape(reach, st, HEAD_DIM)
        )
        for d in range(1, reach + 1):
            part_routes(half, d, lambda copy: copy.start())

    for d in range(1, reach + 1):

        @pl.when(last - me - d == me)
        def _():
            part_in[0, d - 1] = part_out[1, d - 1]

    for half in range(2):
        k_turn = jnp.concatenate([k_buf[half, d].T for d in range(reach + 1)], axis=1)
        v_turn = jnp.concatenate([v_buf[half, d].T for d in range(reach + 1)], axis=1)
        for h in range(0, heads, PAIR):
            cols = slice(h * HEAD_DIM, h * HEAD_DIM + wide)
            att = matmul(v_turn, p_buf[half, :, cols])
            grad = matmul(k_turn, d_buf[half, :, cols]) * scaling
            for j in range(PAIR):
                own = slice(j * HEAD_DIM, (j + 1) * HEAD_DIM)
                out = slice((h + j) * HEAD_DIM, (h + j + 1) * HEAD_DIM)
                att_ref[rows[half], out] = att[:, own].T.astype(jnp.bfloat16)
                dq_ref[rows[half], out] = grad[:, own].T.astype(jnp.bfloat16)

    for half in range(2):
        key_own = matmul(d_buf[half, :st], gather(q_buf, half, 0, heads)) * scaling
        value_own = matmul(p_buf[half, :st], gather(g_buf, half, 0, heads))
        for d in range(1, reach + 1):
            arrives = (last - me - d != me) if half == 0 else (me >= d)

            @pl.when(arrives)
            def _():
                part_copy(half, d, me, half).wait_recv()

        for d in range(reach):
            key_own += part_in[half, d, :st].astype(jnp.float32)
            value_own += part_in[half, d, st:].astype(jnp.float32)
        dk_ref[rows[half]] = key_own.astype(jnp.bfloat16)
        dv_ref[rows[half]] = value_own.astype(jnp.bfloat16)

    kv_routes(lambda copy: copy.wait_send())
    for half in range(2):
        for d in range(1, reach + 1):
            part_routes(half, d, lambda copy: copy.wait_send())


def shards(query_rows, key_rows, value_rows, out_grad, doc_lengths):
    n = lax.axis_size("ctx")
    reach = min(DOC_STRETCHES, n // 4)
    tok, width = query_rows.shape
    st = tok // 2
    heads = width // HEAD_DIM
    low = jnp.bfloat16
    vmem = pl.BlockSpec(memory_space=pltpu.VMEM)
    hbm = pl.BlockSpec(memory_space=pl.ANY)
    like = lambda x: jax.ShapeDtypeStruct(x.shape, low)
    macs = 2 * heads * st * st * (reach + 1) * HEAD_DIM * 6
    return pl.pallas_call(
        functools.partial(kernel, n, reach, heads),
        out_shape=(like(query_rows), like(query_rows), like(key_rows), like(key_rows)),
        in_specs=[pl.BlockSpec(memory_space=pltpu.SMEM), hbm, hbm, hbm, hbm],
        out_specs=(vmem,) * 4,
        scratch_shapes=[
            pltpu.VMEM((2, st, width), low),
            pltpu.VMEM((2, st, width), low),
            pltpu.VMEM((2, reach + 1, st, HEAD_DIM), low),
            pltpu.VMEM((2, reach + 1, st, HEAD_DIM), low),
            pltpu.VMEM((2, st, width), jnp.float32),
            pltpu.VMEM((2, st, width), jnp.float32),
            pltpu.VMEM((2, (reach + 1) * st, width), low),
            pltpu.VMEM((2, (reach + 1) * st, width), low),
            pltpu.VMEM((2, reach, 2 * st, HEAD_DIM), low),
            pltpu.VMEM((2, reach, 2 * st, HEAD_DIM), low),
            pltpu.SemaphoreType.DMA((2, 4)),
            pltpu.SemaphoreType.DMA((2, reach, 2)),
            pltpu.SemaphoreType.DMA((2, reach, 2)),
            pltpu.SemaphoreType.DMA((2, reach)),
            pltpu.SemaphoreType.DMA((2, reach)),
        ],
        compiler_params=pltpu.CompilerParams(
            collective_id=0, has_side_effects=True, vmem_limit_bytes=40 * 1024 * 1024
        ),
        cost_estimate=pl.CostEstimate(
            flops=2 * macs,
            bytes_accessed=8 * tok * width + 8 * tok * HEAD_DIM,
            transcendentals=2 * heads * st * st * reach,
        ),
    )(doc_lengths, query_rows, key_rows, value_rows, out_grad)


def solution(mesh):
    rows = P(("groups", "ctx"), "head")
    return jax.shard_map(
        shards,
        mesh=mesh,
        in_specs=(rows, rows, rows, rows, P("groups")),
        out_specs=(rows,) * 4,
        check_vma=False,
    )
```

```python
import functools
import math

import jax
import jax.numpy as jnp
from jax import lax
from jax.experimental import pallas as pl
from jax.experimental.pallas import tpu as pltpu
from jax.sharding import PartitionSpec as P

HEAD_DIM = 128
DOC_STRETCHES = 8
PAIR = 2
MESH = pl.DeviceIdType.MESH
NT = (((1,), (1,)), ((), ()))


def kernel(
    n,
    reach,
    heads,
    docs_hbm,
    q_hbm,
    k_hbm,
    v_hbm,
    g_hbm,
    att_ref,
    dq_ref,
    dk_ref,
    dv_ref,
    docs_ref,
    q_buf,
    g_buf,
    k_buf,
    v_buf,
    s_own,
    w_own,
    p_buf,
    d_buf,
    part_out,
    part_in,
    docs_sem,
    load_sem,
    kv_send,
    kv_recv,
    part_send,
    part_recv,
):
    st = q_hbm.shape[0] // 2
    me = lax.axis_index("ctx")
    last = 2 * n - 1
    scaling = HEAD_DIM**-0.5
    wide = PAIR * HEAD_DIM
    rows = [slice(half * st, (half + 1) * st) for half in range(2)]
    dot = functools.partial(lax.dot_general, preferred_element_type=jnp.float32)

    def matmul(a, b):
        return dot(a, b, (((1,), (0,)), ((), ())))

    docs_copy = pltpu.make_async_copy(docs_hbm, docs_ref, docs_sem)
    docs_copy.start()
    loads = []
    for half in range(2):
        for slot, (src, dst) in enumerate(
            (
                (k_hbm, k_buf.at[half, 0]),
                (q_hbm, q_buf.at[half]),
                (v_hbm, v_buf.at[half, 0]),
                (g_hbm, g_buf.at[half]),
            )
        ):
            copy = pltpu.make_async_copy(src.at[rows[half]], dst, load_sem.at[half, slot])
            copy.start()
            loads.append(copy)

    barrier = pltpu.get_barrier_semaphore()
    for by in range(1, reach + 1):
        for sign in (-1, 1):
            other = me + sign * by

            @pl.when((other >= 0) & (other < n))
            def _():
                pl.semaphore_signal(
                    barrier, inc=1, device_id={"ctx": other}, device_id_type=MESH
                )

    for d in range(1, reach + 1):

        @pl.when(me < d)
        def _():
            k_buf[0, d] = jnp.zeros_like(k_buf[0, d])
            v_buf[0, d] = jnp.zeros_like(v_buf[0, d])
            part_in[1, d - 1] = jnp.zeros_like(part_in[1, d - 1])

    pl.semaphore_wait(barrier, jnp.minimum(me, reach) + jnp.minimum(n - 1 - me, reach))

    def kv_copies(half, d, target, to_half):
        return [
            pltpu.make_async_remote_copy(
                src_ref=src.at[rows[half]],
                dst_ref=dst.at[to_half, d],
                send_sem=kv_send.at[half, d - 1, which],
                recv_sem=kv_recv.at[to_half, d - 1, which],
                device_id={"ctx": target},
                device_id_type=MESH,
            )
            for which, (src, dst) in enumerate(((k_hbm, k_buf), (v_hbm, v_buf)))
        ]

    def kv_routes(act):
        for d in range(1, reach + 1):
            up = me + d
            fold = last - up

            @pl.when(up < n)
            def _():
                for copy in kv_copies(0, d, up, 0):
                    act(copy)

            @pl.when((up >= n) & (fold != me))
            def _():
                for copy in kv_copies(0, d, fold, 1):
                    act(copy)

            @pl.when(me >= d)
            def _():
                for copy in kv_copies(1, d, me - d, 1):
                    act(copy)

    kv_routes(lambda copy: copy.start())

    docs_copy.wait()

    lane = lax.broadcasted_iota(jnp.int32, (st, st), 1)
    sub = lax.broadcasted_iota(jnp.int32, (st, st), 0)
    lower = sub <= lane
    lower_low = lower.astype(jnp.float32).astype(jnp.bfloat16)
    lower_wide = jnp.concatenate([lower] * PAIR, axis=1)
    lower_low = jnp.concatenate([lower_low] * PAIR, axis=1)
    bias = []
    for half in range(2):
        stretch = me if half == 0 else last - me
        base = stretch * st
        row_pos = base + lane[:8]
        first = jnp.zeros((8, st), jnp.int32)
        begin = jnp.int32(0)
        for i in range(docs_ref.shape[0]):
            first = jnp.where(row_pos >= begin, begin, first)
            begin = begin + docs_ref[i]
        first = first[:1] - base
        blocks = [jnp.where(lower, sub, sub - reach * st)]
        blocks += [sub - d * st for d in range(1, reach)]
        blocks = [jnp.where(block >= first, 0.0, -1e30) for block in blocks]
        bias.append([jnp.concatenate([block] * PAIR, axis=1) for block in blocks])

    def gather(buf, half, first, count):
        cols = [
            buf[half, :, h * HEAD_DIM : (h + 1) * HEAD_DIM] for h in range(first, first + count)
        ]
        return jnp.concatenate(cols, axis=0)

    for copy in loads:
        copy.wait()

    for d in range(1, reach + 1):

        @pl.when(last - me - d == me)
        def _():
            k_buf[1, d] = k_buf[0, 0]
            v_buf[1, d] = v_buf[0, 0]

    for half in range(2):
        for h in range(0, heads, PAIR):
            cols = slice(h * HEAD_DIM, h * HEAD_DIM + wide)
            s_own[half, :, cols] = dot(k_buf[half, 0], gather(q_buf, half, h, PAIR), NT)
            w_own[half, :, cols] = dot(v_buf[half, 0], gather(g_buf, half, h, PAIR), NT)

    def part_copy(half, d, target, to_half):
        return pltpu.make_async_remote_copy(
            src_ref=part_out.at[half, d - 1],
            dst_ref=part_in.at[to_half, d - 1],
            send_sem=part_send.at[half, d - 1],
            recv_sem=part_recv.at[to_half, d - 1],
            device_id={"ctx": target},
            device_id_type=MESH,
        )

    def part_routes(half, d, act):
        if half == 0:

            @pl.when(me >= d)
            def _():
                act(part_copy(0, d, me - d, 0))

        else:
            up = me + d
            fold = last - up

            @pl.when(up < n)
            def _():
                act(part_copy(1, d, up, 1))

            @pl.when((up >= n) & (fold != me))
            def _():
                act(part_copy(1, d, fold, 0))

    def wait_kv(half, d):
        for copy in kv_copies(half, d, me, half):
            copy.wait_recv()

    for half in range(2):
        for d in range(1, reach + 1):
            arrives = (me >= d) if half == 0 else (last - me - d != me)

            @pl.when(arrives)
            def _():
                wait_kv(half, d)

        for h in range(0, heads, PAIR):
            cols = slice(h * HEAD_DIM, h * HEAD_DIM + wide)
            q_cols = gather(q_buf, half, h, PAIR)
            g_cols = gather(g_buf, half, h, PAIR)
            far = dot(k_buf[half, reach], q_cols, NT)
            scores = [jnp.where(lower_wide, s_own[half, :, cols], far)]
            scores += [dot(k_buf[half, d], q_cols, NT) for d in range(1, reach)]
            scores = [score + mask for score, mask in zip(scores, bias[half])]
            top = functools.reduce(jnp.maximum, scores)
            top = jnp.max(top, axis=0, keepdims=True)
            factor = scaling * math.log2(math.e)
            weights = [jnp.exp2((score - top) * factor) for score in scores]
            total = jnp.sum(functools.reduce(jnp.add, weights), axis=0, keepdims=True)
            inverse = 1.0 / total
            weights = [weight * inverse for weight in weights]
            far = dot(v_buf[half, reach], g_cols, NT)
            grads = [jnp.where(lower_wide, w_own[half, :, cols], far)]
            grads += [dot(v_buf[half, d], g_cols, NT) for d in range(1, reach)]
            delta = functools.reduce(jnp.add, [w * g for w, g in zip(weights, grads)])
            delta = jnp.sum(delta, axis=0, keepdims=True)
            for d in range(reach):
                low = weights[d].astype(jnp.bfloat16)
                slope = (weights[d] * (grads[d] - delta)).astype(jnp.bfloat16)
                if d == 0:
                    low_own = low * lower_low
                    slope_own = slope * lower_low
                    p_buf[half, :st, cols] = low_own
                    d_buf[half, :st, cols] = slope_own
                    p_buf[half, reach * st :, cols] = low - low_own
                    d_buf[half, reach * st :, cols] = slope - slope_own
                else:
                    p_buf[half, d * st : (d + 1) * st, cols] = low
                    d_buf[half, d * st : (d + 1) * st, cols] = slope

        part_out[half, :, :st] = (
            (matmul(d_buf[half, st:], gather(q_buf, half, 0, heads)) * scaling)
            .astype(jnp.bfloat16)
            .reshape(reach, st, HEAD_DIM)
        )
        part_out[half, :, st:] = (
            matmul(p_buf[half, st:], gather(g_buf, half, 0, heads))
            .astype(jnp.bfloat16)
            .reshape(reach, st, HEAD_DIM)
        )
        for d in range(1, reach + 1):
            part_routes(half, d, lambda copy: copy.start())

    for d in range(1, reach + 1):

        @pl.when(last - me - d == me)
        def _():
            part_in[0, d - 1] = part_out[1, d - 1]

    for half in range(2):
        k_turn = jnp.concatenate([k_buf[half, d].T for d in range(reach + 1)], axis=1)
        v_turn = jnp.concatenate([v_buf[half, d].T for d in range(reach + 1)], axis=1)
        for h in range(0, heads, PAIR):
            cols = slice(h * HEAD_DIM, h * HEAD_DIM + wide)
            att = matmul(v_turn, p_buf[half, :, cols])
            grad = matmul(k_turn, d_buf[half, :, cols]) * scaling
            for j in range(PAIR):
                own = slice(j * HEAD_DIM, (j + 1) * HEAD_DIM)
                out = slice((h + j) * HEAD_DIM, (h + j + 1) * HEAD_DIM)
                att_ref[rows[half], out] = att[:, own].T.astype(jnp.bfloat16)
                dq_ref[rows[half], out] = grad[:, own].T.astype(jnp.bfloat16)

    for half in range(2):
        key_own = matmul(d_buf[half, :st], gather(q_buf, half, 0, heads)) * scaling
        value_own = matmul(p_buf[half, :st], gather(g_buf, half, 0, heads))
        for d in range(1, reach + 1):
            arrives = (last - me - d != me) if half == 0 else (me >= d)

            @pl.when(arrives)
            def _():
                part_copy(half, d, me, half).wait_recv()

        for d in range(reach):
            key_own += part_in[half, d, :st].astype(jnp.float32)
            value_own += part_in[half, d, st:].astype(jnp.float32)
        dk_ref[rows[half]] = key_own.astype(jnp.bfloat16)
        dv_ref[rows[half]] = value_own.astype(jnp.bfloat16)

    kv_routes(lambda copy: copy.wait_send())
    for half in range(2):
        for d in range(1, reach + 1):
            part_routes(half, d, lambda copy: copy.wait_send())


def write_out(*refs):
    sems = refs[8]
    copies = [pltpu.make_async_copy(refs[i], refs[4 + i], sems.at[i]) for i in range(4)]
    for copy in copies:
        copy.start()
    for copy in copies:
        copy.wait()


def shards(query_rows, key_rows, value_rows, out_grad, doc_lengths):
    n = lax.axis_size("ctx")
    reach = min(DOC_STRETCHES, n // 4)
    tok, width = query_rows.shape
    st = tok // 2
    heads = width // HEAD_DIM
    low = jnp.bfloat16
    vmem = pl.BlockSpec(memory_space=pltpu.VMEM)
    hbm = pl.BlockSpec(memory_space=pltpu.HBM)
    anywhere = pl.BlockSpec(memory_space=pl.ANY)
    like = lambda x: jax.ShapeDtypeStruct(x.shape, low)
    macs = 2 * heads * st * st * (reach + 1) * HEAD_DIM * 6
    shapes = (like(query_rows), like(query_rows), like(key_rows), like(key_rows))
    results = pl.pallas_call(
        functools.partial(kernel, n, reach, heads),
        out_shape=shapes,
        in_specs=[hbm, hbm, hbm, hbm, hbm],
        out_specs=(vmem,) * 4,
        scratch_shapes=[
            pltpu.SMEM(doc_lengths.shape, jnp.int32),
            pltpu.VMEM((2, st, width), low),
            pltpu.VMEM((2, st, width), low),
            pltpu.VMEM((2, reach + 1, st, HEAD_DIM), low),
            pltpu.VMEM((2, reach + 1, st, HEAD_DIM), low),
            pltpu.VMEM((2, st, width), jnp.float32),
            pltpu.VMEM((2, st, width), jnp.float32),
            pltpu.VMEM((2, (reach + 1) * st, width), low),
            pltpu.VMEM((2, (reach + 1) * st, width), low),
            pltpu.VMEM((2, reach, 2 * st, HEAD_DIM), low),
            pltpu.VMEM((2, reach, 2 * st, HEAD_DIM), low),
            pltpu.SemaphoreType.DMA,
            pltpu.SemaphoreType.DMA((2, 4)),
            pltpu.SemaphoreType.DMA((2, reach, 2)),
            pltpu.SemaphoreType.DMA((2, reach, 2)),
            pltpu.SemaphoreType.DMA((2, reach)),
            pltpu.SemaphoreType.DMA((2, reach)),
        ],
        compiler_params=pltpu.CompilerParams(
            collective_id=0, has_side_effects=True, vmem_limit_bytes=40 * 1024 * 1024
        ),
        cost_estimate=pl.CostEstimate(
            flops=2 * macs,
            bytes_accessed=8 * tok * width + 8 * tok * HEAD_DIM,
            transcendentals=2 * heads * st * st * reach,
        ),
    )(*[
        pltpu.with_memory_space_constraint(x, pltpu.HBM)
        for x in (doc_lengths, query_rows, key_rows, value_rows, out_grad)
    ])
    return pl.pallas_call(
        write_out,
        out_shape=shapes,
        in_specs=[anywhere] * 4,
        out_specs=(hbm,) * 4,
        scratch_shapes=[pltpu.SemaphoreType.DMA((4,))],
    )(*results)


def solution(mesh):
    rows = P(("groups", "ctx"), "head")
    return jax.shard_map(
        shards,
        mesh=mesh,
        in_specs=(rows, rows, rows, rows, P("groups")),
        out_specs=(rows,) * 4,
        check_vma=False,
    )
```

```python
import functools
import math

import jax
import jax.numpy as jnp
from jax import lax
from jax.experimental import pallas as pl
from jax.experimental.pallas import tpu as pltpu
from jax.sharding import PartitionSpec as P

HEAD_DIM = 128
DOC_STRETCHES = 8
PAIR = 2
MESH = pl.DeviceIdType.MESH
NT = (((1,), (1,)), ((), ()))


def kernel(
    n,
    reach,
    heads,
    docs_hbm,
    q_hbm,
    k_hbm,
    v_hbm,
    g_hbm,
    att_ref,
    dq_ref,
    dk_ref,
    dv_ref,
    docs_ref,
    q_buf,
    g_buf,
    k_buf,
    v_buf,
    s_own,
    w_own,
    w_buf,
    p_buf,
    d_buf,
    part_out,
    part_in,
    docs_sem,
    load_sem,
    kv_send,
    kv_recv,
    part_send,
    part_recv,
):
    st = q_hbm.shape[0] // 2
    me = lax.axis_index("ctx")
    last = 2 * n - 1
    scaling = HEAD_DIM**-0.5
    wide = PAIR * HEAD_DIM
    rows = [slice(half * st, (half + 1) * st) for half in range(2)]
    dot = functools.partial(lax.dot_general, preferred_element_type=jnp.float32)

    def matmul(a, b):
        return dot(a, b, (((1,), (0,)), ((), ())))

    barrier = pltpu.get_barrier_semaphore()
    for by in range(1, reach + 1):
        for sign in (-1, 1):
            other = me + sign * by

            @pl.when((other >= 0) & (other < n))
            def _():
                pl.semaphore_signal(
                    barrier, inc=1, device_id={"ctx": other}, device_id_type=MESH
                )

    docs_copy = pltpu.make_async_copy(docs_hbm, docs_ref, docs_sem)
    docs_copy.start()
    loads = []
    for half in range(2):
        for slot, (src, dst) in enumerate(
            (
                (k_hbm, k_buf.at[half, 0]),
                (q_hbm, q_buf.at[half]),
                (v_hbm, v_buf.at[half, 0]),
                (g_hbm, g_buf.at[half]),
            )
        ):
            copy = pltpu.make_async_copy(src.at[rows[half]], dst, load_sem.at[half, slot])
            copy.start()
            loads.append(copy)

    for d in range(1, reach + 1):

        @pl.when(me < d)
        def _():
            k_buf[0, d] = jnp.zeros_like(k_buf[0, d])
            v_buf[0, d] = jnp.zeros_like(v_buf[0, d])
            part_in[:, 1, d - 1] = jnp.zeros_like(part_in[:, 1, d - 1])

        @pl.when((me + d >= n) & (last - me - d > me))
        def _():
            part_in[:, 0, d - 1] = jnp.zeros_like(part_in[:, 0, d - 1])

    docs_copy.wait()

    lane = lax.broadcasted_iota(jnp.int32, (st, st), 1)
    sub = lax.broadcasted_iota(jnp.int32, (st, st), 0)
    lower = sub <= lane
    lower_low = lower.astype(jnp.float32).astype(jnp.bfloat16)
    lower_wide = jnp.concatenate([lower] * PAIR, axis=1)
    lower_low = jnp.concatenate([lower_low] * PAIR, axis=1)
    bias = []
    for half in range(2):
        stretch = me if half == 0 else last - me
        base = stretch * st
        row_pos = base + lane[:8]
        first = jnp.zeros((8, st), jnp.int32)
        begin = jnp.int32(0)
        for i in range(docs_ref.shape[0]):
            first = jnp.where(row_pos >= begin, begin, first)
            begin = begin + docs_ref[i]
        first = first[:1] - base
        blocks = [jnp.where(lower, sub, sub - reach * st)]
        blocks += [sub - d * st for d in range(1, reach)]
        blocks = [jnp.where(block >= first, 0.0, -1e30) for block in blocks]
        bias.append([jnp.concatenate([block] * PAIR, axis=1) for block in blocks])

    pl.semaphore_wait(barrier, jnp.minimum(me, reach) + jnp.minimum(n - 1 - me, reach))

    def kv_copy(which, half, d, target, to_half):
        src, dst = ((k_hbm, k_buf), (v_hbm, v_buf))[which]
        return pltpu.make_async_remote_copy(
            src_ref=src.at[rows[half]],
            dst_ref=dst.at[to_half, d],
            send_sem=kv_send.at[half, d - 1, which],
            recv_sem=kv_recv.at[to_half, d - 1, which],
            device_id={"ctx": target},
            device_id_type=MESH,
        )

    def kv_routes(which, act):
        for d in range(1, reach + 1):
            up = me + d
            fold = last - up

            @pl.when(me >= d)
            def _():
                act(kv_copy(which, 1, d, me - d, 1))

            @pl.when(up < n)
            def _():
                act(kv_copy(which, 0, d, up, 0))

            @pl.when((up >= n) & (fold < me))
            def _():
                act(kv_copy(which, 0, d, fold, 1))

    def kv_arrive(which):
        buf = (k_buf, v_buf)[which]
        for d in range(1, reach + 1):

            @pl.when(me >= d)
            def _():
                kv_copy(which, 0, d, me, 0).wait_recv()

        for d in range(1, reach + 1):
            source = last - me - d

            @pl.when(source > me)
            def _():
                kv_copy(which, 1, d, me, 1).wait_recv()

            @pl.when(source <= me)
            def _():
                buf[1, d] = buf[0, me - source]

    kv_routes(0, lambda copy: copy.start())
    kv_routes(1, lambda copy: copy.start())

    def gather(buf, half, first, count):
        cols = [
            buf[half, :, h * HEAD_DIM : (h + 1) * HEAD_DIM] for h in range(first, first + count)
        ]
        return jnp.concatenate(cols, axis=0)

    for copy in loads:
        copy.wait()

    for half in (1, 0):
        for h in range(0, heads, PAIR):
            cols = slice(h * HEAD_DIM, h * HEAD_DIM + wide)
            s_own[half, :, cols] = dot(k_buf[half, 0], gather(q_buf, half, h, PAIR), NT)
            w_own[half, :, cols] = dot(v_buf[half, 0], gather(g_buf, half, h, PAIR), NT)

    def part_copy(which, half, d, target, to_half):
        return pltpu.make_async_remote_copy(
            src_ref=part_out.at[which, half, d - 1],
            dst_ref=part_in.at[which, to_half, d - 1],
            send_sem=part_send.at[which, half, d - 1],
            recv_sem=part_recv.at[which, to_half, d - 1],
            device_id={"ctx": target},
            device_id_type=MESH,
        )

    def part_routes(which, half, act):
        for d in range(1, reach + 1):
            up = me + d
            fold = last - up
            if half == 0:

                @pl.when(me >= d)
                def _():
                    act(part_copy(which, 0, d, me - d, 0))

            else:

                @pl.when(up < n)
                def _():
                    act(part_copy(which, 1, d, up, 1))

                @pl.when((up >= n) & (fold > me))
                def _():
                    act(part_copy(which, 1, d, fold, 0))

    def give_back(which, half, parts):
        part_out[which, half] = parts.astype(jnp.bfloat16).reshape(reach, st, HEAD_DIM)
        for d in range(1, reach + 1):
            if half == 0:
                twin = last - 2 * me + d

                @pl.when(twin <= reach)
                def _():
                    both = part_out[which, 0, d - 1].astype(jnp.float32)
                    both += part_out[which, 1, twin - 1].astype(jnp.float32)
                    part_out[which, 0, d - 1] = both.astype(jnp.bfloat16)

            else:

                @pl.when(last - me - d == me)
                def _():
                    part_in[which, 0, d - 1] = part_out[which, 1, d - 1]

        part_routes(which, half, lambda copy: copy.start())

    kv_arrive(0)
    factor = scaling * math.log2(math.e)
    for half in (1, 0):
        for h in range(0, heads, PAIR):
            cols = slice(h * HEAD_DIM, h * HEAD_DIM + wide)
            q_cols = gather(q_buf, half, h, PAIR)
            far = dot(k_buf[half, reach], q_cols, NT)
            scores = [jnp.where(lower_wide, s_own[half, :, cols], far)]
            scores += [dot(k_buf[half, d], q_cols, NT) for d in range(1, reach)]
            scores = [score + mask for score, mask in zip(scores, bias[half])]
            top = functools.reduce(jnp.maximum, scores)
            top = jnp.max(top, axis=0, keepdims=True)
            weights = [jnp.exp2((score - top) * factor) for score in scores]
            total = jnp.sum(functools.reduce(jnp.add, weights), axis=0, keepdims=True)
            inverse = 1.0 / total
            for d in range(reach):
                weight = weights[d] * inverse
                w_buf[half, d, :, cols] = weight
                low = weight.astype(jnp.bfloat16)
                if d == 0:
                    low_own = low * lower_low
                    p_buf[half, :st, cols] = low_own
                    p_buf[half, reach * st :, cols] = low - low_own
                else:
                    p_buf[half, d * st : (d + 1) * st, cols] = low
        give_back(1, half, matmul(p_buf[half, st:], gather(g_buf, half, 0, heads)))

    kv_arrive(1)
    for half in (1, 0):
        for h in range(0, heads, PAIR):
            cols = slice(h * HEAD_DIM, h * HEAD_DIM + wide)
            g_cols = gather(g_buf, half, h, PAIR)
            far = dot(v_buf[half, reach], g_cols, NT)
            grads = [jnp.where(lower_wide, w_own[half, :, cols], far)]
            grads += [dot(v_buf[half, d], g_cols, NT) for d in range(1, reach)]
            weights = [w_buf[half, d, :, cols] for d in range(reach)]
            delta = functools.reduce(jnp.add, [w * g for w, g in zip(weights, grads)])
            delta = jnp.sum(delta, axis=0, keepdims=True)
            for d in range(reach):
                slope = (weights[d] * (grads[d] - delta)).astype(jnp.bfloat16)
                if d == 0:
                    slope_own = slope * lower_low
                    d_buf[half, :st, cols] = slope_own
                    d_buf[half, reach * st :, cols] = slope - slope_own
                else:
                    d_buf[half, d * st : (d + 1) * st, cols] = slope
        give_back(0, half, matmul(d_buf[half, st:], gather(q_buf, half, 0, heads)) * scaling)

    for half in (1, 0):
        k_turn = jnp.concatenate([k_buf[half, d].T for d in range(reach + 1)], axis=1)
        v_turn = jnp.concatenate([v_buf[half, d].T for d in range(reach + 1)], axis=1)
        for h in range(0, heads, PAIR):
            cols = slice(h * HEAD_DIM, h * HEAD_DIM + wide)
            att = matmul(v_turn, p_buf[half, :, cols])
            grad = matmul(k_turn, d_buf[half, :, cols]) * scaling
            for j in range(PAIR):
                own = slice(j * HEAD_DIM, (j + 1) * HEAD_DIM)
                out = slice((h + j) * HEAD_DIM, (h + j + 1) * HEAD_DIM)
                att_ref[rows[half], out] = att[:, own].T.astype(jnp.bfloat16)
                dq_ref[rows[half], out] = grad[:, own].T.astype(jnp.bfloat16)

    for which, half in ((1, 1), (1, 0), (0, 1), (0, 0)):
        if which == 0:
            own = matmul(d_buf[half, :st], gather(q_buf, half, 0, heads)) * scaling
        else:
            own = matmul(p_buf[half, :st], gather(g_buf, half, 0, heads))
        for d in range(1, reach + 1):
            arrives = ((me + d < n) | (last - me - d < me)) if half == 0 else (me >= d)

            @pl.when(arrives)
            def _():
                part_copy(which, half, d, me, half).wait_recv()

        for d in range(reach):
            own += part_in[which, half, d].astype(jnp.float32)
        (dk_ref, dv_ref)[which][rows[half]] = own.astype(jnp.bfloat16)

    for which in range(2):
        kv_routes(which, lambda copy: copy.wait_send())
        for half in range(2):
            part_routes(which, half, lambda copy: copy.wait_send())


def write_out(*refs):
    sems = refs[8]
    copies = [pltpu.make_async_copy(refs[i], refs[4 + i], sems.at[i]) for i in range(4)]
    for copy in copies:
        copy.start()
    for copy in copies:
        copy.wait()


def shards(query_rows, key_rows, value_rows, out_grad, doc_lengths):
    n = lax.axis_size("ctx")
    reach = min(DOC_STRETCHES, n // 4)
    tok, width = query_rows.shape
    st = tok // 2
    heads = width // HEAD_DIM
    low = jnp.bfloat16
    vmem = pl.BlockSpec(memory_space=pltpu.VMEM)
    hbm = pl.BlockSpec(memory_space=pltpu.HBM)
    anywhere = pl.BlockSpec(memory_space=pl.ANY)
    like = lambda x: jax.ShapeDtypeStruct(x.shape, low)
    macs = 2 * heads * st * st * (reach + 1) * HEAD_DIM * 6
    shapes = (like(query_rows), like(query_rows), like(key_rows), like(key_rows))
    results = pl.pallas_call(
        functools.partial(kernel, n, reach, heads),
        out_shape=shapes,
        in_specs=[hbm, hbm, hbm, hbm, hbm],
        out_specs=(vmem,) * 4,
        scratch_shapes=[
            pltpu.SMEM(doc_lengths.shape, jnp.int32),
            pltpu.VMEM((2, st, width), low),
            pltpu.VMEM((2, st, width), low),
            pltpu.VMEM((2, reach + 1, st, HEAD_DIM), low),
            pltpu.VMEM((2, reach + 1, st, HEAD_DIM), low),
            pltpu.VMEM((2, st, width), jnp.float32),
            pltpu.VMEM((2, st, width), jnp.float32),
            pltpu.VMEM((2, reach, st, width), jnp.float32),
            pltpu.VMEM((2, (reach + 1) * st, width), low),
            pltpu.VMEM((2, (reach + 1) * st, width), low),
            pltpu.VMEM((2, 2, reach, st, HEAD_DIM), low),
            pltpu.VMEM((2, 2, reach, st, HEAD_DIM), low),
            pltpu.SemaphoreType.DMA,
            pltpu.SemaphoreType.DMA((2, 4)),
            pltpu.SemaphoreType.DMA((2, reach, 2)),
            pltpu.SemaphoreType.DMA((2, reach, 2)),
            pltpu.SemaphoreType.DMA((2, 2, reach)),
            pltpu.SemaphoreType.DMA((2, 2, reach)),
        ],
        compiler_params=pltpu.CompilerParams(
            collective_id=0, has_side_effects=True, vmem_limit_bytes=40 * 1024 * 1024
        ),
        cost_estimate=pl.CostEstimate(
            flops=2 * macs,
            bytes_accessed=8 * tok * width + 8 * tok * HEAD_DIM,
            transcendentals=2 * heads * st * st * reach,
        ),
    )(*[
        pltpu.with_memory_space_constraint(x, pltpu.HBM)
        for x in (doc_lengths, query_rows, key_rows, value_rows, out_grad)
    ])
    return pl.pallas_call(
        write_out,
        out_shape=shapes,
        in_specs=[anywhere] * 4,
        out_specs=(hbm,) * 4,
        scratch_shapes=[pltpu.SemaphoreType.DMA((4,))],
        compiler_params=pltpu.CompilerParams(vmem_limit_bytes=4 * 1024 * 1024),
    )(*results)


def solution(mesh):
    rows = P(("groups", "ctx"), "head")
    return jax.shard_map(
        shards,
        mesh=mesh,
        in_specs=(rows, rows, rows, rows, P("groups")),
        out_specs=(rows,) * 4,
        check_vma=False,
    )
```

```python
import functools
import math

import jax
import jax.numpy as jnp
from jax import lax
from jax.experimental import pallas as pl
from jax.experimental.pallas import tpu as pltpu
from jax.sharding import PartitionSpec as P

HEAD_DIM = 128
DOC_STRETCHES = 8
PAIR = 2
MESH = pl.DeviceIdType.MESH
NT = (((1,), (1,)), ((), ()))


def kernel(
    n,
    reach,
    heads,
    docs_hbm,
    q_hbm,
    k_hbm,
    v_hbm,
    g_hbm,
    att_ref,
    dq_ref,
    dk_ref,
    dv_ref,
    docs_ref,
    q_buf,
    g_buf,
    k_buf,
    v_buf,
    s_own,
    w_own,
    p_buf,
    d_buf,
    part_out,
    part_in,
    docs_sem,
    load_sem,
    kv_send,
    kv_recv,
    part_send,
    part_recv,
):
    st = q_hbm.shape[0] // 2
    me = lax.axis_index("ctx")
    last = 2 * n - 1
    scaling = HEAD_DIM**-0.5
    wide = PAIR * HEAD_DIM
    rows = [slice(half * st, (half + 1) * st) for half in range(2)]
    dot = functools.partial(lax.dot_general, preferred_element_type=jnp.float32)

    def matmul(a, b):
        return dot(a, b, (((1,), (0,)), ((), ())))

    barrier = pltpu.get_barrier_semaphore()
    for by in range(1, reach + 1):
        for sign in (-1, 1):
            other = me + sign * by

            @pl.when((other >= 0) & (other < n))
            def _():
                pl.semaphore_signal(
                    barrier, inc=1, device_id={"ctx": other}, device_id_type=MESH
                )

    docs_copy = pltpu.make_async_copy(docs_hbm, docs_ref, docs_sem)
    docs_copy.start()
    loads = []
    for half in range(2):
        for slot, (src, dst) in enumerate(
            (
                (k_hbm, k_buf.at[half, 0]),
                (q_hbm, q_buf.at[half]),
                (v_hbm, v_buf.at[half, 0]),
                (g_hbm, g_buf.at[half]),
            )
        ):
            copy = pltpu.make_async_copy(src.at[rows[half]], dst, load_sem.at[half, slot])
            copy.start()
            loads.append(copy)

    for d in range(1, reach + 1):

        @pl.when(me < d)
        def _():
            k_buf[0, d] = jnp.zeros_like(k_buf[0, d])
            v_buf[0, d] = jnp.zeros_like(v_buf[0, d])
            part_in[1, d - 1] = jnp.zeros_like(part_in[1, d - 1])

        @pl.when((me + d >= n) & (last - me - d > me))
        def _():
            part_in[0, d - 1] = jnp.zeros_like(part_in[0, d - 1])

    docs_copy.wait()

    lane = lax.broadcasted_iota(jnp.int32, (st, st), 1)
    sub = lax.broadcasted_iota(jnp.int32, (st, st), 0)
    lower = sub <= lane
    lower_low = lower.astype(jnp.float32).astype(jnp.bfloat16)
    lower_wide = jnp.concatenate([lower] * PAIR, axis=1)
    lower_low = jnp.concatenate([lower_low] * PAIR, axis=1)
    bias = []
    for half in range(2):
        stretch = me if half == 0 else last - me
        base = stretch * st
        row_pos = base + lane[:8]
        first = jnp.zeros((8, st), jnp.int32)
        begin = jnp.int32(0)
        for i in range(docs_ref.shape[0]):
            first = jnp.where(row_pos >= begin, begin, first)
            begin = begin + docs_ref[i]
        first = first[:1] - base
        blocks = [jnp.where(lower, sub, sub - reach * st)]
        blocks += [sub - d * st for d in range(1, reach)]
        blocks = [jnp.where(block >= first, 0.0, -1e30) for block in blocks]
        bias.append([jnp.concatenate([block] * PAIR, axis=1) for block in blocks])

    pl.semaphore_wait(barrier, jnp.minimum(me, reach) + jnp.minimum(n - 1 - me, reach))

    def kv_copy(which, half, d, target, to_half):
        src, dst = ((k_hbm, k_buf), (v_hbm, v_buf))[which]
        return pltpu.make_async_remote_copy(
            src_ref=src.at[rows[half]],
            dst_ref=dst.at[to_half, d],
            send_sem=kv_send.at[half, d - 1, which],
            recv_sem=kv_recv.at[to_half, d - 1, which],
            device_id={"ctx": target},
            device_id_type=MESH,
        )

    def kv_routes(half, act):
        for d in range(1, reach + 1):
            up = me + d
            fold = last - up
            for which in range(2):
                if half == 1:

                    @pl.when(me >= d)
                    def _():
                        act(kv_copy(which, 1, d, me - d, 1))

                else:

                    @pl.when(up < n)
                    def _():
                        act(kv_copy(which, 0, d, up, 0))

                    @pl.when((up >= n) & (fold < me))
                    def _():
                        act(kv_copy(which, 0, d, fold, 1))

    def kv_arrive(half):
        for d in range(1, reach + 1):
            source = last - me - d
            for which in range(2):
                arrives = (me >= d) if half == 0 else (source > me)

                @pl.when(arrives)
                def _():
                    kv_copy(which, half, d, me, half).wait_recv()

    for half in (1, 0):
        kv_routes(half, lambda copy: copy.start())

    def gather(buf, half, first, count):
        cols = [
            buf[half, :, h * HEAD_DIM : (h + 1) * HEAD_DIM] for h in range(first, first + count)
        ]
        return jnp.concatenate(cols, axis=0)

    for copy in loads:
        copy.wait()

    for half in (1, 0):
        for h in range(0, heads, PAIR):
            cols = slice(h * HEAD_DIM, h * HEAD_DIM + wide)
            s_own[half, :, cols] = dot(k_buf[half, 0], gather(q_buf, half, h, PAIR), NT)
            w_own[half, :, cols] = dot(v_buf[half, 0], gather(g_buf, half, h, PAIR), NT)

    def part_copy(half, d, target, to_half):
        return pltpu.make_async_remote_copy(
            src_ref=part_out.at[half, d - 1],
            dst_ref=part_in.at[to_half, d - 1],
            send_sem=part_send.at[half, d - 1],
            recv_sem=part_recv.at[to_half, d - 1],
            device_id={"ctx": target},
            device_id_type=MESH,
        )

    def part_routes(half, act):
        for d in range(1, reach + 1):
            up = me + d
            fold = last - up
            if half == 0:

                @pl.when(me >= d)
                def _():
                    act(part_copy(0, d, me - d, 0))

            else:

                @pl.when(up < n)
                def _():
                    act(part_copy(1, d, up, 1))

                @pl.when((up >= n) & (fold > me))
                def _():
                    act(part_copy(1, d, fold, 0))

    def give_back(half):
        for d in range(1, reach + 1):
            if half == 0:
                twin = last - 2 * me + d

                @pl.when(twin <= reach)
                def _():
                    both = part_out[0, d - 1].astype(jnp.float32)
                    both += part_out[1, twin - 1].astype(jnp.float32)
                    part_out[0, d - 1] = both.astype(jnp.bfloat16)

            else:

                @pl.when(last - me - d == me)
                def _():
                    part_in[0, d - 1] = part_out[1, d - 1]

        part_routes(half, lambda copy: copy.start())

    kv_arrive(1)
    crosses = last - 2 * me <= reach

    @pl.when(crosses)
    def _():
        kv_arrive(0)

    for d in range(1, reach + 1):
        source = last - me - d

        @pl.when(source <= me)
        def _():
            k_buf[1, d] = k_buf[0, me - source]
            v_buf[1, d] = v_buf[0, me - source]

    factor = scaling * math.log2(math.e)
    for half in (1, 0):
        if half == 0:

            @pl.when(jnp.logical_not(crosses))
            def _():
                kv_arrive(0)

        k_rest = k_buf[half, 1:].reshape(reach * st, HEAD_DIM)
        v_rest = v_buf[half, 1:].reshape(reach * st, HEAD_DIM)
        for h in range(0, heads, PAIR):
            cols = slice(h * HEAD_DIM, h * HEAD_DIM + wide)

            def blocks(own, rest):
                merged = jnp.where(lower_wide, own[half, :, cols], rest[(reach - 1) * st :])
                return [merged] + [rest[(d - 1) * st : d * st] for d in range(1, reach)]

            scores = blocks(s_own, dot(k_rest, gather(q_buf, half, h, PAIR), NT))
            scores = [score + mask for score, mask in zip(scores, bias[half])]
            top = functools.reduce(jnp.maximum, scores)
            top = jnp.max(top, axis=0, keepdims=True)
            weights = [jnp.exp2((score - top) * factor) for score in scores]
            total = jnp.sum(functools.reduce(jnp.add, weights), axis=0, keepdims=True)
            inverse = 1.0 / total
            weights = [weight * inverse for weight in weights]
            grads = blocks(w_own, dot(v_rest, gather(g_buf, half, h, PAIR), NT))
            delta = functools.reduce(jnp.add, [w * g for w, g in zip(weights, grads)])
            delta = jnp.sum(delta, axis=0, keepdims=True)
            for d in range(reach):
                low = weights[d].astype(jnp.bfloat16)
                slope = (weights[d] * (grads[d] - delta)).astype(jnp.bfloat16)
                if d == 0:
                    low_own = low * lower_low
                    slope_own = slope * lower_low
                    p_buf[half, :st, cols] = low_own
                    d_buf[half, :st, cols] = slope_own
                    p_buf[half, reach * st :, cols] = low - low_own
                    d_buf[half, reach * st :, cols] = slope - slope_own
                else:
                    p_buf[half, d * st : (d + 1) * st, cols] = low
                    d_buf[half, d * st : (d + 1) * st, cols] = slope

        part_out[half, :, :st] = (
            (matmul(d_buf[half, st:], gather(q_buf, half, 0, heads)) * scaling)
            .astype(jnp.bfloat16)
            .reshape(reach, st, HEAD_DIM)
        )
        part_out[half, :, st:] = (
            matmul(p_buf[half, st:], gather(g_buf, half, 0, heads))
            .astype(jnp.bfloat16)
            .reshape(reach, st, HEAD_DIM)
        )
        give_back(half)

    for half in (1, 0):
        k_turn = jnp.concatenate([k_buf[half, d].T for d in range(reach + 1)], axis=1)
        v_turn = jnp.concatenate([v_buf[half, d].T for d in range(reach + 1)], axis=1)
        for h in range(0, heads, PAIR):
            cols = slice(h * HEAD_DIM, h * HEAD_DIM + wide)
            att = matmul(v_turn, p_buf[half, :, cols])
            grad = matmul(k_turn, d_buf[half, :, cols]) * scaling
            for j in range(PAIR):
                own = slice(j * HEAD_DIM, (j + 1) * HEAD_DIM)
                out = slice((h + j) * HEAD_DIM, (h + j + 1) * HEAD_DIM)
                att_ref[rows[half], out] = att[:, own].T.astype(jnp.bfloat16)
                dq_ref[rows[half], out] = grad[:, own].T.astype(jnp.bfloat16)

    for half in (1, 0):
        key_own = matmul(d_buf[half, :st], gather(q_buf, half, 0, heads)) * scaling
        value_own = matmul(p_buf[half, :st], gather(g_buf, half, 0, heads))
        for d in range(1, reach + 1):
            arrives = ((me + d < n) | (last - me - d < me)) if half == 0 else (me >= d)

            @pl.when(arrives)
            def _():
                part_copy(half, d, me, half).wait_recv()

        for d in range(reach):
            key_own += part_in[half, d, :st].astype(jnp.float32)
            value_own += part_in[half, d, st:].astype(jnp.float32)
        dk_ref[rows[half]] = key_own.astype(jnp.bfloat16)
        dv_ref[rows[half]] = value_own.astype(jnp.bfloat16)

    for half in (1, 0):
        kv_routes(half, lambda copy: copy.wait_send())
        part_routes(half, lambda copy: copy.wait_send())


def write_out(*refs):
    sems = refs[8]
    copies = [pltpu.make_async_copy(refs[i], refs[4 + i], sems.at[i]) for i in range(4)]
    for copy in copies:
        copy.start()
    for copy in copies:
        copy.wait()


def shards(query_rows, key_rows, value_rows, out_grad, doc_lengths):
    n = lax.axis_size("ctx")
    reach = min(DOC_STRETCHES, n // 4)
    tok, width = query_rows.shape
    st = tok // 2
    heads = width // HEAD_DIM
    low = jnp.bfloat16
    vmem = pl.BlockSpec(memory_space=pltpu.VMEM)
    hbm = pl.BlockSpec(memory_space=pltpu.HBM)
    anywhere = pl.BlockSpec(memory_space=pl.ANY)
    like = lambda x: jax.ShapeDtypeStruct(x.shape, low)
    macs = 2 * heads * st * st * (reach + 1) * HEAD_DIM * 6
    shapes = (like(query_rows), like(query_rows), like(key_rows), like(key_rows))
    results = pl.pallas_call(
        functools.partial(kernel, n, reach, heads),
        out_shape=shapes,
        in_specs=[hbm, hbm, hbm, hbm, hbm],
        out_specs=(vmem,) * 4,
        scratch_shapes=[
            pltpu.SMEM(doc_lengths.shape, jnp.int32),
            pltpu.VMEM((2, st, width), low),
            pltpu.VMEM((2, st, width), low),
            pltpu.VMEM((2, reach + 1, st, HEAD_DIM), low),
            pltpu.VMEM((2, reach + 1, st, HEAD_DIM), low),
            pltpu.VMEM((2, st, width), jnp.float32),
            pltpu.VMEM((2, st, width), jnp.float32),
            pltpu.VMEM((2, (reach + 1) * st, width), low),
            pltpu.VMEM((2, (reach + 1) * st, width), low),
            pltpu.VMEM((2, reach, 2 * st, HEAD_DIM), low),
            pltpu.VMEM((2, reach, 2 * st, HEAD_DIM), low),
            pltpu.SemaphoreType.DMA,
            pltpu.SemaphoreType.DMA((2, 4)),
            pltpu.SemaphoreType.DMA((2, reach, 2)),
            pltpu.SemaphoreType.DMA((2, reach, 2)),
            pltpu.SemaphoreType.DMA((2, reach)),
            pltpu.SemaphoreType.DMA((2, reach)),
        ],
        compiler_params=pltpu.CompilerParams(
            collective_id=0, has_side_effects=True, vmem_limit_bytes=40 * 1024 * 1024
        ),
        cost_estimate=pl.CostEstimate(
            flops=2 * macs,
            bytes_accessed=8 * tok * width + 8 * tok * HEAD_DIM,
            transcendentals=2 * heads * st * st * reach,
        ),
    )(*[
        pltpu.with_memory_space_constraint(x, pltpu.HBM)
        for x in (doc_lengths, query_rows, key_rows, value_rows, out_grad)
    ])
    return pl.pallas_call(
        write_out,
        out_shape=shapes,
        in_specs=[anywhere] * 4,
        out_specs=(hbm,) * 4,
        scratch_shapes=[pltpu.SemaphoreType.DMA((4,))],
        compiler_params=pltpu.CompilerParams(vmem_limit_bytes=4 * 1024 * 1024),
    )(*results)


def solution(mesh):
    rows = P(("groups", "ctx"), "head")
    return jax.shard_map(
        shards,
        mesh=mesh,
        in_specs=(rows, rows, rows, rows, P("groups")),
        out_specs=(rows,) * 4,
        check_vma=False,
    )
```

```python
import functools
import math

import jax
import jax.numpy as jnp
from jax import lax
from jax.experimental import pallas as pl
from jax.experimental.pallas import tpu as pltpu
from jax.sharding import PartitionSpec as P

HEAD_DIM = 128
DOC_STRETCHES = 8
PAIR = 2
MESH = pl.DeviceIdType.MESH
NT = (((1,), (1,)), ((), ()))


def kernel(
    n,
    reach,
    heads,
    docs_hbm,
    q_hbm,
    k_hbm,
    v_hbm,
    g_hbm,
    att_ref,
    dq_ref,
    dk_ref,
    dv_ref,
    docs_ref,
    q_buf,
    g_buf,
    k_buf,
    v_buf,
    s_own,
    w_own,
    w_buf,
    p_buf,
    d_buf,
    part_out,
    part_in,
    docs_sem,
    load_sem,
    kv_send,
    kv_recv,
    part_send,
    part_recv,
):
    st = q_hbm.shape[0] // 2
    me = lax.axis_index("ctx")
    last = 2 * n - 1
    scaling = HEAD_DIM**-0.5
    wide = PAIR * HEAD_DIM
    rows = [slice(half * st, (half + 1) * st) for half in range(2)]
    dot = functools.partial(lax.dot_general, preferred_element_type=jnp.float32)

    def matmul(a, b):
        return dot(a, b, (((1,), (0,)), ((), ())))

    barrier = pltpu.get_barrier_semaphore()
    for by in range(1, reach + 1):
        for sign in (-1, 1):
            other = me + sign * by

            @pl.when((other >= 0) & (other < n))
            def _():
                pl.semaphore_signal(
                    barrier, inc=1, device_id={"ctx": other}, device_id_type=MESH
                )

    docs_copy = pltpu.make_async_copy(docs_hbm, docs_ref, docs_sem)
    docs_copy.start()
    loads = []
    for half in range(2):
        for slot, (src, dst) in enumerate(
            (
                (k_hbm, k_buf.at[half, 0]),
                (q_hbm, q_buf.at[half]),
                (v_hbm, v_buf.at[half, 0]),
                (g_hbm, g_buf.at[half]),
            )
        ):
            copy = pltpu.make_async_copy(src.at[rows[half]], dst, load_sem.at[half, slot])
            copy.start()
            loads.append(copy)

    for d in range(1, reach + 1):

        @pl.when(me < d)
        def _():
            k_buf[0, d] = jnp.zeros_like(k_buf[0, d])
            v_buf[0, d] = jnp.zeros_like(v_buf[0, d])
            part_in[:, 1, d - 1] = jnp.zeros_like(part_in[:, 1, d - 1])

        @pl.when((me + d >= n) & (last - me - d > me))
        def _():
            part_in[:, 0, d - 1] = jnp.zeros_like(part_in[:, 0, d - 1])

    pl.semaphore_wait(barrier, jnp.minimum(me, reach) + jnp.minimum(n - 1 - me, reach))

    def kv_copy(which, half, d, target, to_half):
        src, dst = ((k_hbm, k_buf), (v_hbm, v_buf))[which]
        return pltpu.make_async_remote_copy(
            src_ref=src.at[rows[half]],
            dst_ref=dst.at[to_half, d],
            send_sem=kv_send.at[half, d - 1, which],
            recv_sem=kv_recv.at[to_half, d - 1, which],
            device_id={"ctx": target},
            device_id_type=MESH,
        )

    def kv_routes(which, act):
        for d in range(1, reach + 1):
            up = me + d
            fold = last - up

            @pl.when(me >= d)
            def _():
                act(kv_copy(which, 1, d, me - d, 1))

            @pl.when(up < n)
            def _():
                act(kv_copy(which, 0, d, up, 0))

            @pl.when((up >= n) & (fold < me))
            def _():
                act(kv_copy(which, 0, d, fold, 1))

    def kv_arrive(which):
        buf = (k_buf, v_buf)[which]
        for d in range(1, reach + 1):

            @pl.when(me >= d)
            def _():
                kv_copy(which, 0, d, me, 0).wait_recv()

        for d in range(1, reach + 1):
            source = last - me - d

            @pl.when(source > me)
            def _():
                kv_copy(which, 1, d, me, 1).wait_recv()

            @pl.when(source <= me)
            def _():
                buf[1, d] = buf[0, me - source]

    kv_routes(0, lambda copy: copy.start())
    kv_routes(1, lambda copy: copy.start())

    docs_copy.wait()

    lane = lax.broadcasted_iota(jnp.int32, (st, st), 1)
    sub = lax.broadcasted_iota(jnp.int32, (st, st), 0)
    lower = sub <= lane
    lower_low = lower.astype(jnp.float32).astype(jnp.bfloat16)
    lower_wide = jnp.concatenate([lower] * PAIR, axis=1)
    lower_low = jnp.concatenate([lower_low] * PAIR, axis=1)
    bias = []
    for half in range(2):
        stretch = me if half == 0 else last - me
        base = stretch * st
        row_pos = base + lane[:8]
        first = jnp.zeros((8, st), jnp.int32)
        begin = jnp.int32(0)
        for i in range(docs_ref.shape[0]):
            first = jnp.where(row_pos >= begin, begin, first)
            begin = begin + docs_ref[i]
        first = first[:1] - base
        blocks = [jnp.where(lower, sub, sub - reach * st)]
        blocks += [sub - d * st for d in range(1, reach)]
        blocks = [jnp.where(block >= first, 0.0, -1e30) for block in blocks]
        bias.append([jnp.concatenate([block] * PAIR, axis=1) for block in blocks])

    def gather(buf, half, first, count):
        cols = [
            buf[half, :, h * HEAD_DIM : (h + 1) * HEAD_DIM] for h in range(first, first + count)
        ]
        return jnp.concatenate(cols, axis=0)

    for copy in loads:
        copy.wait()

    for half in (1, 0):
        for h in range(0, heads, PAIR):
            cols = slice(h * HEAD_DIM, h * HEAD_DIM + wide)
            s_own[half, :, cols] = dot(k_buf[half, 0], gather(q_buf, half, h, PAIR), NT)
            w_own[half, :, cols] = dot(v_buf[half, 0], gather(g_buf, half, h, PAIR), NT)

    def part_copy(which, half, d, target, to_half):
        return pltpu.make_async_remote_copy(
            src_ref=part_out.at[which, half, d - 1],
            dst_ref=part_in.at[which, to_half, d - 1],
            send_sem=part_send.at[which, half, d - 1],
            recv_sem=part_recv.at[which, to_half, d - 1],
            device_id={"ctx": target},
            device_id_type=MESH,
        )

    def part_routes(which, half, act):
        for d in range(1, reach + 1):
            up = me + d
            fold = last - up
            if half == 0:

                @pl.when(me >= d)
                def _():
                    act(part_copy(which, 0, d, me - d, 0))

            else:

                @pl.when(up < n)
                def _():
                    act(part_copy(which, 1, d, up, 1))

                @pl.when((up >= n) & (fold > me))
                def _():
                    act(part_copy(which, 1, d, fold, 0))

    def give_back(which, half, parts):
        part_out[which, half] = parts.astype(jnp.bfloat16).reshape(reach, st, HEAD_DIM)
        for d in range(1, reach + 1):
            if half == 0:
                twin = last - 2 * me + d

                @pl.when(twin <= reach)
                def _():
                    both = part_out[which, 0, d - 1].astype(jnp.float32)
                    both += part_out[which, 1, twin - 1].astype(jnp.float32)
                    part_out[which, 0, d - 1] = both.astype(jnp.bfloat16)

            else:

                @pl.when(last - me - d == me)
                def _():
                    part_in[which, 0, d - 1] = part_out[which, 1, d - 1]

        part_routes(which, half, lambda copy: copy.start())

    def blocks(own, others):
        merged = jnp.where(lower_wide, own, others[(reach - 1) * st :])
        return [merged] + [others[(d - 1) * st : d * st] for d in range(1, reach)]

    kv_arrive(0)
    factor = scaling * math.log2(math.e)
    for half in (1, 0):
        rest = k_buf[half, 1:].reshape(reach * st, HEAD_DIM)
        for h in range(0, heads, PAIR):
            cols = slice(h * HEAD_DIM, h * HEAD_DIM + wide)
            q_cols = gather(q_buf, half, h, PAIR)
            scores = blocks(s_own[half, :, cols], dot(rest, q_cols, NT))
            scores = [score + mask for score, mask in zip(scores, bias[half])]
            top = functools.reduce(jnp.maximum, scores)
            top = jnp.max(top, axis=0, keepdims=True)
            weights = [jnp.exp2((score - top) * factor) for score in scores]
            total = jnp.sum(functools.reduce(jnp.add, weights), axis=0, keepdims=True)
            inverse = 1.0 / total
            for d in range(reach):
                weight = weights[d] * inverse
                w_buf[half, d, :, cols] = weight
                low = weight.astype(jnp.bfloat16)
                if d == 0:
                    low_own = low * lower_low
                    p_buf[half, :st, cols] = low_own
                    p_buf[half, reach * st :, cols] = low - low_own
                else:
                    p_buf[half, d * st : (d + 1) * st, cols] = low
        give_back(1, half, matmul(p_buf[half, st:], gather(g_buf, half, 0, heads)))

    kv_arrive(1)
    for half in (1, 0):
        rest = v_buf[half, 1:].reshape(reach * st, HEAD_DIM)
        for h in range(0, heads, PAIR):
            cols = slice(h * HEAD_DIM, h * HEAD_DIM + wide)
            g_cols = gather(g_buf, half, h, PAIR)
            grads = blocks(w_own[half, :, cols], dot(rest, g_cols, NT))
            weights = [w_buf[half, d, :, cols] for d in range(reach)]
            delta = functools.reduce(jnp.add, [w * g for w, g in zip(weights, grads)])
            delta = jnp.sum(delta, axis=0, keepdims=True)
            for d in range(reach):
                slope = (weights[d] * (grads[d] - delta)).astype(jnp.bfloat16)
                if d == 0:
                    slope_own = slope * lower_low
                    d_buf[half, :st, cols] = slope_own
                    d_buf[half, reach * st :, cols] = slope - slope_own
                else:
                    d_buf[half, d * st : (d + 1) * st, cols] = slope
        give_back(0, half, matmul(d_buf[half, st:], gather(q_buf, half, 0, heads)) * scaling)

    for half in (1, 0):
        k_turn = jnp.concatenate([k_buf[half, d].T for d in range(reach + 1)], axis=1)
        v_turn = jnp.concatenate([v_buf[half, d].T for d in range(reach + 1)], axis=1)
        for h in range(0, heads, PAIR):
            cols = slice(h * HEAD_DIM, h * HEAD_DIM + wide)
            att = matmul(v_turn, p_buf[half, :, cols])
            grad = matmul(k_turn, d_buf[half, :, cols]) * scaling
            for j in range(PAIR):
                own = slice(j * HEAD_DIM, (j + 1) * HEAD_DIM)
                out = slice((h + j) * HEAD_DIM, (h + j + 1) * HEAD_DIM)
                att_ref[rows[half], out] = att[:, own].T.astype(jnp.bfloat16)
                dq_ref[rows[half], out] = grad[:, own].T.astype(jnp.bfloat16)

    for which, half in ((1, 1), (1, 0), (0, 1), (0, 0)):
        if which == 0:
            own = matmul(d_buf[half, :st], gather(q_buf, half, 0, heads)) * scaling
        else:
            own = matmul(p_buf[half, :st], gather(g_buf, half, 0, heads))
        for d in range(1, reach + 1):
            arrives = ((me + d < n) | (last - me - d < me)) if half == 0 else (me >= d)

            @pl.when(arrives)
            def _():
                part_copy(which, half, d, me, half).wait_recv()

        for d in range(reach):
            own += part_in[which, half, d].astype(jnp.float32)
        (dk_ref, dv_ref)[which][rows[half]] = own.astype(jnp.bfloat16)

    for which in range(2):
        kv_routes(which, lambda copy: copy.wait_send())
        for half in range(2):
            part_routes(which, half, lambda copy: copy.wait_send())


def write_out(*refs):
    sems = refs[8]
    copies = [pltpu.make_async_copy(refs[i], refs[4 + i], sems.at[i]) for i in range(4)]
    for copy in copies:
        copy.start()
    for copy in copies:
        copy.wait()


def shards(query_rows, key_rows, value_rows, out_grad, doc_lengths):
    n = lax.axis_size("ctx")
    reach = min(DOC_STRETCHES, n // 4)
    tok, width = query_rows.shape
    st = tok // 2
    heads = width // HEAD_DIM
    low = jnp.bfloat16
    vmem = pl.BlockSpec(memory_space=pltpu.VMEM)
    hbm = pl.BlockSpec(memory_space=pltpu.HBM)
    anywhere = pl.BlockSpec(memory_space=pl.ANY)
    like = lambda x: jax.ShapeDtypeStruct(x.shape, low)
    macs = 2 * heads * st * st * (reach + 1) * HEAD_DIM * 6
    shapes = (like(query_rows), like(query_rows), like(key_rows), like(key_rows))
    results = pl.pallas_call(
        functools.partial(kernel, n, reach, heads),
        out_shape=shapes,
        in_specs=[hbm, hbm, hbm, hbm, hbm],
        out_specs=(vmem,) * 4,
        scratch_shapes=[
            pltpu.SMEM(doc_lengths.shape, jnp.int32),
            pltpu.VMEM((2, st, width), low),
            pltpu.VMEM((2, st, width), low),
            pltpu.VMEM((2, reach + 1, st, HEAD_DIM), low),
            pltpu.VMEM((2, reach + 1, st, HEAD_DIM), low),
            pltpu.VMEM((2, st, width), jnp.float32),
            pltpu.VMEM((2, st, width), jnp.float32),
            pltpu.VMEM((2, reach, st, width), jnp.float32),
            pltpu.VMEM((2, (reach + 1) * st, width), low),
            pltpu.VMEM((2, (reach + 1) * st, width), low),
            pltpu.VMEM((2, 2, reach, st, HEAD_DIM), low),
            pltpu.VMEM((2, 2, reach, st, HEAD_DIM), low),
            pltpu.SemaphoreType.DMA,
            pltpu.SemaphoreType.DMA((2, 4)),
            pltpu.SemaphoreType.DMA((2, reach, 2)),
            pltpu.SemaphoreType.DMA((2, reach, 2)),
            pltpu.SemaphoreType.DMA((2, 2, reach)),
            pltpu.SemaphoreType.DMA((2, 2, reach)),
        ],
        compiler_params=pltpu.CompilerParams(
            collective_id=0, has_side_effects=True, vmem_limit_bytes=40 * 1024 * 1024
        ),
        cost_estimate=pl.CostEstimate(
            flops=2 * macs,
            bytes_accessed=8 * tok * width + 8 * tok * HEAD_DIM,
            transcendentals=2 * heads * st * st * reach,
        ),
    )(*[
        pltpu.with_memory_space_constraint(x, pltpu.HBM)
        for x in (doc_lengths, query_rows, key_rows, value_rows, out_grad)
    ])
    return pl.pallas_call(
        write_out,
        out_shape=shapes,
        in_specs=[anywhere] * 4,
        out_specs=(hbm,) * 4,
        scratch_shapes=[pltpu.SemaphoreType.DMA((4,))],
        compiler_params=pltpu.CompilerParams(vmem_limit_bytes=4 * 1024 * 1024),
    )(*results)


def solution(mesh):
    rows = P(("groups", "ctx"), "head")
    return jax.shard_map(
        shards,
        mesh=mesh,
        in_specs=(rows, rows, rows, rows, P("groups")),
        out_specs=(rows,) * 4,
        check_vma=False,
    )
```

```python
import functools
import math

import jax
import jax.numpy as jnp
from jax import lax
from jax.experimental import pallas as pl
from jax.experimental.pallas import tpu as pltpu
from jax.sharding import PartitionSpec as P

HEAD_DIM = 128
DOC_STRETCHES = 8
PAIR = 2
MESH = pl.DeviceIdType.MESH
NT = (((1,), (1,)), ((), ()))


def kernel(
    n,
    reach,
    heads,
    docs_hbm,
    q_hbm,
    k_hbm,
    v_hbm,
    g_hbm,
    att_ref,
    dq_ref,
    dk_ref,
    dv_ref,
    docs_ref,
    q_buf,
    g_buf,
    k_buf,
    v_buf,
    s_own,
    w_own,
    p_buf,
    d_buf,
    part_out,
    part_in,
    docs_sem,
    load_sem,
    kv_send,
    kv_recv,
    part_send,
    part_recv,
):
    st = q_hbm.shape[0] // 2
    me = lax.axis_index("ctx")
    last = 2 * n - 1
    scaling = HEAD_DIM**-0.5
    wide = PAIR * HEAD_DIM
    rows = [slice(half * st, (half + 1) * st) for half in range(2)]
    dot = functools.partial(lax.dot_general, preferred_element_type=jnp.float32)

    def matmul(a, b):
        return dot(a, b, (((1,), (0,)), ((), ())))

    barrier = pltpu.get_barrier_semaphore()
    for by in range(1, reach + 1):
        for sign in (-1, 1):
            other = me + sign * by

            @pl.when((other >= 0) & (other < n))
            def _():
                pl.semaphore_signal(
                    barrier, inc=1, device_id={"ctx": other}, device_id_type=MESH
                )

    docs_copy = pltpu.make_async_copy(docs_hbm, docs_ref, docs_sem)
    docs_copy.start()
    loads = []
    for half in range(2):
        for slot, (src, dst) in enumerate(
            (
                (k_hbm, k_buf.at[half, 0]),
                (q_hbm, q_buf.at[half]),
                (v_hbm, v_buf.at[half, 0]),
                (g_hbm, g_buf.at[half]),
            )
        ):
            copy = pltpu.make_async_copy(src.at[rows[half]], dst, load_sem.at[half, slot])
            copy.start()
            loads.append(copy)

    for d in range(1, reach + 1):

        @pl.when(me < d)
        def _():
            k_buf[0, d] = jnp.zeros_like(k_buf[0, d])
            v_buf[0, d] = jnp.zeros_like(v_buf[0, d])
            part_in[1, d - 1] = jnp.zeros_like(part_in[1, d - 1])

        @pl.when((me + d < n) & (last - 2 * me - d <= reach))
        def _():
            part_in[0, d - 1] = jnp.zeros_like(part_in[0, d - 1])

    pl.semaphore_wait(barrier, jnp.minimum(me, reach) + jnp.minimum(n - 1 - me, reach))

    def kv_copy(which, half, d, target, to_half):
        src, dst = ((k_hbm, k_buf), (v_hbm, v_buf))[which]
        return pltpu.make_async_remote_copy(
            src_ref=src.at[rows[half]],
            dst_ref=dst.at[to_half, d],
            send_sem=kv_send.at[half, d - 1, which],
            recv_sem=kv_recv.at[to_half, d - 1, which],
            device_id={"ctx": target},
            device_id_type=MESH,
        )

    def kv_routes(act):
        for d in range(1, reach + 1):
            up = me + d
            fold = last - up

            @pl.when(up < n)
            def _():
                for which in range(2):
                    act(kv_copy(which, 0, d, up, 0))

            @pl.when((up >= n) & (fold < me))
            def _():
                for which in range(2):
                    act(kv_copy(which, 0, d, fold, 1))

            @pl.when(me >= d)
            def _():
                for which in range(2):
                    act(kv_copy(which, 1, d, me - d, 1))

    def kv_arrive(half):
        for d in range(1, reach + 1):
            source = last - me - d
            for which in range(2):
                arrives = (me >= d) if half == 0 else (source > me)

                @pl.when(arrives)
                def _():
                    kv_copy(which, half, d, me, half).wait_recv()

    kv_routes(lambda copy: copy.start())

    docs_copy.wait()

    lane = lax.broadcasted_iota(jnp.int32, (st, st), 1)
    sub = lax.broadcasted_iota(jnp.int32, (st, st), 0)
    lower = sub <= lane
    lower_low = lower.astype(jnp.float32).astype(jnp.bfloat16)
    lower_wide = jnp.concatenate([lower] * PAIR, axis=1)
    lower_low = jnp.concatenate([lower_low] * PAIR, axis=1)
    bias = []
    for half in range(2):
        stretch = me if half == 0 else last - me
        base = stretch * st
        row_pos = base + lane[:8]
        first = jnp.zeros((8, st), jnp.int32)
        begin = jnp.int32(0)
        for i in range(docs_ref.shape[0]):
            first = jnp.where(row_pos >= begin, begin, first)
            begin = begin + docs_ref[i]
        first = first[:1] - base
        blocks = [jnp.where(lower, sub, sub - reach * st)]
        blocks += [sub - d * st for d in range(1, reach)]
        blocks = [jnp.where(block >= first, 0.0, -1e30) for block in blocks]
        bias.append([jnp.concatenate([block] * PAIR, axis=1) for block in blocks])

    def gather(buf, half, first, count):
        cols = [
            buf[half, :, h * HEAD_DIM : (h + 1) * HEAD_DIM] for h in range(first, first + count)
        ]
        return jnp.concatenate(cols, axis=0)

    for copy in loads:
        copy.wait()

    for half in (0, 1):
        for h in range(0, heads, PAIR):
            cols = slice(h * HEAD_DIM, h * HEAD_DIM + wide)
            s_own[half, :, cols] = dot(k_buf[half, 0], gather(q_buf, half, h, PAIR), NT)
            w_own[half, :, cols] = dot(v_buf[half, 0], gather(g_buf, half, h, PAIR), NT)

    def part_copy(half, d, target, to_half):
        return pltpu.make_async_remote_copy(
            src_ref=part_out.at[half, d - 1],
            dst_ref=part_in.at[to_half, d - 1],
            send_sem=part_send.at[half, d - 1],
            recv_sem=part_recv.at[to_half, d - 1],
            device_id={"ctx": target},
            device_id_type=MESH,
        )

    def part_routes(half, act):
        for d in range(1, reach + 1):
            up = me + d
            fold = last - up
            if half == 0:

                @pl.when((me >= d) & (last - 2 * me + d > reach))
                def _():
                    act(part_copy(0, d, me - d, 0))

            else:

                @pl.when(up < n)
                def _():
                    act(part_copy(1, d, up, 1))

                @pl.when((up >= n) & (fold != me))
                def _():
                    act(part_copy(1, d, fold, 0))

    def give_back(half):
        if half == 1:
            for d in range(1, reach + 1):
                fold = last - me - d

                @pl.when(fold < me)
                def _():
                    both = part_out[1, d - 1].astype(jnp.float32)
                    both += part_out[0, me - fold - 1].astype(jnp.float32)
                    part_out[1, d - 1] = both.astype(jnp.bfloat16)

                @pl.when(fold == me)
                def _():
                    part_in[0, d - 1] = part_out[1, d - 1]

        part_routes(half, lambda copy: copy.start())

    factor = scaling * math.log2(math.e)
    for half in (0, 1):
        kv_arrive(half)
        if half == 1:
            for d in range(1, reach + 1):
                source = last - me - d

                @pl.when(source <= me)
                def _():
                    k_buf[1, d] = k_buf[0, me - source]
                    v_buf[1, d] = v_buf[0, me - source]

        k_rest = k_buf[half, 1:].reshape(reach * st, HEAD_DIM)
        v_rest = v_buf[half, 1:].reshape(reach * st, HEAD_DIM)
        for h in range(0, heads, PAIR):
            cols = slice(h * HEAD_DIM, h * HEAD_DIM + wide)

            def blocks(own, rest):
                merged = jnp.where(lower_wide, own[half, :, cols], rest[(reach - 1) * st :])
                return [merged] + [rest[(d - 1) * st : d * st] for d in range(1, reach)]

            scores = blocks(s_own, dot(k_rest, gather(q_buf, half, h, PAIR), NT))
            scores = [score + mask for score, mask in zip(scores, bias[half])]
            top = functools.reduce(jnp.maximum, scores)
            top = jnp.max(top, axis=0, keepdims=True)
            weights = [jnp.exp2((score - top) * factor) for score in scores]
            total = jnp.sum(functools.reduce(jnp.add, weights), axis=0, keepdims=True)
            inverse = 1.0 / total
            weights = [weight * inverse for weight in weights]
            grads = blocks(w_own, dot(v_rest, gather(g_buf, half, h, PAIR), NT))
            delta = functools.reduce(jnp.add, [w * g for w, g in zip(weights, grads)])
            delta = jnp.sum(delta, axis=0, keepdims=True)
            for d in range(reach):
                low = weights[d].astype(jnp.bfloat16)
                slope = (weights[d] * (grads[d] - delta)).astype(jnp.bfloat16)
                if d == 0:
                    low_own = low * lower_low
                    slope_own = slope * lower_low
                    p_buf[half, :st, cols] = low_own
                    d_buf[half, :st, cols] = slope_own
                    p_buf[half, reach * st :, cols] = low - low_own
                    d_buf[half, reach * st :, cols] = slope - slope_own
                else:
                    p_buf[half, d * st : (d + 1) * st, cols] = low
                    d_buf[half, d * st : (d + 1) * st, cols] = slope

        part_out[half, :, :st] = (
            (matmul(d_buf[half, st:], gather(q_buf, half, 0, heads)) * scaling)
            .astype(jnp.bfloat16)
            .reshape(reach, st, HEAD_DIM)
        )
        part_out[half, :, st:] = (
            matmul(p_buf[half, st:], gather(g_buf, half, 0, heads))
            .astype(jnp.bfloat16)
            .reshape(reach, st, HEAD_DIM)
        )
        give_back(half)

    for half in (0, 1):
        k_turn = jnp.concatenate([k_buf[half, d].T for d in range(reach + 1)], axis=1)
        v_turn = jnp.concatenate([v_buf[half, d].T for d in range(reach + 1)], axis=1)
        for h in range(0, heads, PAIR):
            cols = slice(h * HEAD_DIM, h * HEAD_DIM + wide)
            att = matmul(v_turn, p_buf[half, :, cols])
            grad = matmul(k_turn, d_buf[half, :, cols]) * scaling
            for j in range(PAIR):
                own = slice(j * HEAD_DIM, (j + 1) * HEAD_DIM)
                out = slice((h + j) * HEAD_DIM, (h + j + 1) * HEAD_DIM)
                att_ref[rows[half], out] = att[:, own].T.astype(jnp.bfloat16)
                dq_ref[rows[half], out] = grad[:, own].T.astype(jnp.bfloat16)

    for half in (0, 1):
        key_own = matmul(d_buf[half, :st], gather(q_buf, half, 0, heads)) * scaling
        value_own = matmul(p_buf[half, :st], gather(g_buf, half, 0, heads))
        for d in range(1, reach + 1):
            arrives = me >= d
            if half == 0:
                joined = (me + d < n) & (last - 2 * me - d <= reach)
                arrives = jnp.logical_not(joined) & (last - me - d != me)

            @pl.when(arrives)
            def _():
                part_copy(half, d, me, half).wait_recv()

        for d in range(reach):
            key_own += part_in[half, d, :st].astype(jnp.float32)
            value_own += part_in[half, d, st:].astype(jnp.float32)
        dk_ref[rows[half]] = key_own.astype(jnp.bfloat16)
        dv_ref[rows[half]] = value_own.astype(jnp.bfloat16)

    kv_routes(lambda copy: copy.wait_send())
    for half in (0, 1):
        part_routes(half, lambda copy: copy.wait_send())


def write_out(*refs):
    sems = refs[8]
    copies = [pltpu.make_async_copy(refs[i], refs[4 + i], sems.at[i]) for i in range(4)]
    for copy in copies:
        copy.start()
    for copy in copies:
        copy.wait()


def shards(query_rows, key_rows, value_rows, out_grad, doc_lengths):
    n = lax.axis_size("ctx")
    reach = min(DOC_STRETCHES, n // 4)
    tok, width = query_rows.shape
    st = tok // 2
    heads = width // HEAD_DIM
    low = jnp.bfloat16
    vmem = pl.BlockSpec(memory_space=pltpu.VMEM)
    hbm = pl.BlockSpec(memory_space=pltpu.HBM)
    anywhere = pl.BlockSpec(memory_space=pl.ANY)
    like = lambda x: jax.ShapeDtypeStruct(x.shape, low)
    macs = 2 * heads * st * st * (reach + 1) * HEAD_DIM * 6
    shapes = (like(query_rows), like(query_rows), like(key_rows), like(key_rows))
    results = pl.pallas_call(
        functools.partial(kernel, n, reach, heads),
        out_shape=shapes,
        in_specs=[hbm, hbm, hbm, hbm, hbm],
        out_specs=(vmem,) * 4,
        scratch_shapes=[
            pltpu.SMEM(doc_lengths.shape, jnp.int32),
            pltpu.VMEM((2, st, width), low),
            pltpu.VMEM((2, st, width), low),
            pltpu.VMEM((2, reach + 1, st, HEAD_DIM), low),
            pltpu.VMEM((2, reach + 1, st, HEAD_DIM), low),
            pltpu.VMEM((2, st, width), jnp.float32),
            pltpu.VMEM((2, st, width), jnp.float32),
            pltpu.VMEM((2, (reach + 1) * st, width), low),
            pltpu.VMEM((2, (reach + 1) * st, width), low),
            pltpu.VMEM((2, reach, 2 * st, HEAD_DIM), low),
            pltpu.VMEM((2, reach, 2 * st, HEAD_DIM), low),
            pltpu.SemaphoreType.DMA,
            pltpu.SemaphoreType.DMA((2, 4)),
            pltpu.SemaphoreType.DMA((2, reach, 2)),
            pltpu.SemaphoreType.DMA((2, reach, 2)),
            pltpu.SemaphoreType.DMA((2, reach)),
            pltpu.SemaphoreType.DMA((2, reach)),
        ],
        compiler_params=pltpu.CompilerParams(
            collective_id=0, has_side_effects=True, vmem_limit_bytes=40 * 1024 * 1024
        ),
        cost_estimate=pl.CostEstimate(
            flops=2 * macs,
            bytes_accessed=8 * tok * width + 8 * tok * HEAD_DIM,
            transcendentals=2 * heads * st * st * reach,
        ),
    )(*[
        pltpu.with_memory_space_constraint(x, pltpu.HBM)
        for x in (doc_lengths, query_rows, key_rows, value_rows, out_grad)
    ])
    return pl.pallas_call(
        write_out,
        out_shape=shapes,
        in_specs=[anywhere] * 4,
        out_specs=(hbm,) * 4,
        scratch_shapes=[pltpu.SemaphoreType.DMA((4,))],
        compiler_params=pltpu.CompilerParams(vmem_limit_bytes=4 * 1024 * 1024),
    )(*results)


def solution(mesh):
    rows = P(("groups", "ctx"), "head")
    return jax.shard_map(
        shards,
        mesh=mesh,
        in_specs=(rows, rows, rows, rows, P("groups")),
        out_specs=(rows,) * 4,
        check_vma=False,
    )
```

```python
import functools
import math

import jax
import jax.numpy as jnp
from jax import lax
from jax.experimental import pallas as pl
from jax.experimental.pallas import tpu as pltpu
from jax.sharding import PartitionSpec as P

HEAD_DIM = 128
DOC_STRETCHES = 8
PAIR = 2
MESH = pl.DeviceIdType.MESH
NT = (((1,), (1,)), ((), ()))


def kernel(
    n,
    reach,
    heads,
    docs_hbm,
    q_hbm,
    k_hbm,
    v_hbm,
    g_hbm,
    att_ref,
    dq_ref,
    dk_ref,
    dv_ref,
    docs_ref,
    q_buf,
    g_buf,
    k_buf,
    v_buf,
    s_own,
    w_own,
    p_buf,
    d_buf,
    part_out,
    part_in,
    docs_sem,
    load_sem,
    kv_send,
    kv_recv,
    part_send,
    part_recv,
):
    st = q_hbm.shape[0] // 2
    me = lax.axis_index("ctx")
    last = 2 * n - 1
    scaling = HEAD_DIM**-0.5
    wide = PAIR * HEAD_DIM
    rows = [slice(half * st, (half + 1) * st) for half in range(2)]
    dot = functools.partial(lax.dot_general, preferred_element_type=jnp.float32)

    def matmul(a, b):
        return dot(a, b, (((1,), (0,)), ((), ())))

    barrier = pltpu.get_barrier_semaphore()
    for by in range(1, reach + 1):
        for sign in (-1, 1):
            other = me + sign * by

            @pl.when((other >= 0) & (other < n))
            def _():
                pl.semaphore_signal(
                    barrier, inc=1, device_id={"ctx": other}, device_id_type=MESH
                )

    docs_copy = pltpu.make_async_copy(docs_hbm, docs_ref, docs_sem)
    docs_copy.start()
    loads = []
    for half in range(2):
        for slot, (src, dst) in enumerate(
            (
                (k_hbm, k_buf.at[half, 0]),
                (q_hbm, q_buf.at[half]),
                (v_hbm, v_buf.at[half, 0]),
                (g_hbm, g_buf.at[half]),
            )
        ):
            copy = pltpu.make_async_copy(src.at[rows[half]], dst, load_sem.at[half, slot])
            copy.start()
            loads.append(copy)

    for d in range(1, reach + 1):

        @pl.when(me < d)
        def _():
            k_buf[0, d] = jnp.zeros_like(k_buf[0, d])
            v_buf[0, d] = jnp.zeros_like(v_buf[0, d])
            part_in[1, d - 1] = jnp.zeros_like(part_in[1, d - 1])

        @pl.when((me + d < n) & (last - 2 * me - d <= reach))
        def _():
            part_in[0, d - 1] = jnp.zeros_like(part_in[0, d - 1])

    pl.semaphore_wait(barrier, jnp.minimum(me, reach) + jnp.minimum(n - 1 - me, reach))

    def kv_copy(which, half, d, target, to_half):
        src, dst = ((k_hbm, k_buf), (v_hbm, v_buf))[which]
        return pltpu.make_async_remote_copy(
            src_ref=src.at[rows[half]],
            dst_ref=dst.at[to_half, d],
            send_sem=kv_send.at[half, d - 1, which],
            recv_sem=kv_recv.at[to_half, d - 1, which],
            device_id={"ctx": target},
            device_id_type=MESH,
        )

    def kv_routes(to_half, act):
        for d in range(1, reach + 1):
            up = me + d
            fold = last - up
            if to_half == 0:

                @pl.when(up < n)
                def _():
                    for which in range(2):
                        act(kv_copy(which, 0, d, up, 0))

            else:

                @pl.when((up >= n) & (fold < me))
                def _():
                    for which in range(2):
                        act(kv_copy(which, 0, d, fold, 1))

                @pl.when(me >= d)
                def _():
                    for which in range(2):
                        act(kv_copy(which, 1, d, me - d, 1))

    def kv_arrive(half):
        for d in range(1, reach + 1):
            source = last - me - d
            for which in range(2):
                arrives = (me >= d) if half == 0 else (source > me)

                @pl.when(arrives)
                def _():
                    kv_copy(which, half, d, me, half).wait_recv()

    kv_routes(0, lambda copy: copy.start())

    docs_copy.wait()

    lane = lax.broadcasted_iota(jnp.int32, (st, st), 1)
    sub = lax.broadcasted_iota(jnp.int32, (st, st), 0)
    lower = sub <= lane
    lower_low = lower.astype(jnp.float32).astype(jnp.bfloat16)
    lower_wide = jnp.concatenate([lower] * PAIR, axis=1)
    lower_low = jnp.concatenate([lower_low] * PAIR, axis=1)
    bias = []
    for half in range(2):
        stretch = me if half == 0 else last - me
        base = stretch * st
        row_pos = base + lane[:8]
        first = jnp.zeros((8, st), jnp.int32)
        begin = jnp.int32(0)
        for i in range(docs_ref.shape[0]):
            first = jnp.where(row_pos >= begin, begin, first)
            begin = begin + docs_ref[i]
        first = first[:1] - base
        blocks = [jnp.where(lower, sub, sub - reach * st)]
        blocks += [sub - d * st for d in range(1, reach)]
        blocks = [jnp.where(block >= first, 0.0, -1e30) for block in blocks]
        bias.append([jnp.concatenate([block] * PAIR, axis=1) for block in blocks])

    def gather(buf, half, first, count):
        cols = [
            buf[half, :, h * HEAD_DIM : (h + 1) * HEAD_DIM] for h in range(first, first + count)
        ]
        return jnp.concatenate(cols, axis=0)

    for half in (0, 1):
        for copy in loads[4 * half : 4 * half + 4]:
            copy.wait()
        if half == 1:
            kv_routes(1, lambda copy: copy.start())
        for h in range(0, heads, PAIR):
            cols = slice(h * HEAD_DIM, h * HEAD_DIM + wide)
            s_own[half, :, cols] = dot(k_buf[half, 0], gather(q_buf, half, h, PAIR), NT)
            w_own[half, :, cols] = dot(v_buf[half, 0], gather(g_buf, half, h, PAIR), NT)

    def part_copy(half, d, target, to_half):
        return pltpu.make_async_remote_copy(
            src_ref=part_out.at[half, d - 1],
            dst_ref=part_in.at[to_half, d - 1],
            send_sem=part_send.at[half, d - 1],
            recv_sem=part_recv.at[to_half, d - 1],
            device_id={"ctx": target},
            device_id_type=MESH,
        )

    def part_routes(half, act):
        for d in range(1, reach + 1):
            up = me + d
            fold = last - up
            if half == 0:

                @pl.when((me >= d) & (last - 2 * me + d > reach))
                def _():
                    act(part_copy(0, d, me - d, 0))

            else:

                @pl.when(up < n)
                def _():
                    act(part_copy(1, d, up, 1))

                @pl.when((up >= n) & (fold != me))
                def _():
                    act(part_copy(1, d, fold, 0))

    def give_back(half):
        if half == 1:
            for d in range(1, reach + 1):
                fold = last - me - d

                @pl.when(fold < me)
                def _():
                    both = part_out[1, d - 1].astype(jnp.float32)
                    both += part_out[0, me - fold - 1].astype(jnp.float32)
                    part_out[1, d - 1] = both.astype(jnp.bfloat16)

                @pl.when(fold == me)
                def _():
                    part_in[0, d - 1] = part_out[1, d - 1]

        part_routes(half, lambda copy: copy.start())

    factor = scaling * math.log2(math.e)
    for half in (0, 1):
        kv_arrive(half)
        if half == 1:
            for d in range(1, reach + 1):
                source = last - me - d

                @pl.when(source <= me)
                def _():
                    k_buf[1, d] = k_buf[0, me - source]
                    v_buf[1, d] = v_buf[0, me - source]

        k_rest = k_buf[half, 1:].reshape(reach * st, HEAD_DIM)
        v_rest = v_buf[half, 1:].reshape(reach * st, HEAD_DIM)
        for h in range(0, heads, PAIR):
            cols = slice(h * HEAD_DIM, h * HEAD_DIM + wide)

            def blocks(own, rest):
                merged = jnp.where(lower_wide, own[half, :, cols], rest[(reach - 1) * st :])
                return [merged] + [rest[(d - 1) * st : d * st] for d in range(1, reach)]

            scores = blocks(s_own, dot(k_rest, gather(q_buf, half, h, PAIR), NT))
            scores = [score + mask for score, mask in zip(scores, bias[half])]
            top = functools.reduce(jnp.maximum, scores)
            top = jnp.max(top, axis=0, keepdims=True)
            weights = [jnp.exp2((score - top) * factor) for score in scores]
            total = jnp.sum(functools.reduce(jnp.add, weights), axis=0, keepdims=True)
            inverse = 1.0 / total
            weights = [weight * inverse for weight in weights]
            grads = blocks(w_own, dot(v_rest, gather(g_buf, half, h, PAIR), NT))
            delta = functools.reduce(jnp.add, [w * g for w, g in zip(weights, grads)])
            delta = jnp.sum(delta, axis=0, keepdims=True)
            for d in range(reach):
                low = weights[d].astype(jnp.bfloat16)
                slope = (weights[d] * (grads[d] - delta)).astype(jnp.bfloat16)
                if d == 0:
                    low_own = low * lower_low
                    slope_own = slope * lower_low
                    p_buf[half, :st, cols] = low_own
                    d_buf[half, :st, cols] = slope_own
                    p_buf[half, reach * st :, cols] = low - low_own
                    d_buf[half, reach * st :, cols] = slope - slope_own
                else:
                    p_buf[half, d * st : (d + 1) * st, cols] = low
                    d_buf[half, d * st : (d + 1) * st, cols] = slope

        part_out[half, :, :st] = (
            (matmul(d_buf[half, st:], gather(q_buf, half, 0, heads)) * scaling)
            .astype(jnp.bfloat16)
            .reshape(reach, st, HEAD_DIM)
        )
        part_out[half, :, st:] = (
            matmul(p_buf[half, st:], gather(g_buf, half, 0, heads))
            .astype(jnp.bfloat16)
            .reshape(reach, st, HEAD_DIM)
        )
        give_back(half)

    for half in (0, 1):
        k_turn = jnp.concatenate([k_buf[half, d].T for d in range(reach + 1)], axis=1)
        v_turn = jnp.concatenate([v_buf[half, d].T for d in range(reach + 1)], axis=1)
        for h in range(0, heads, PAIR):
            cols = slice(h * HEAD_DIM, h * HEAD_DIM + wide)
            att = matmul(v_turn, p_buf[half, :, cols])
            grad = matmul(k_turn, d_buf[half, :, cols]) * scaling
            for j in range(PAIR):
                own = slice(j * HEAD_DIM, (j + 1) * HEAD_DIM)
                out = slice((h + j) * HEAD_DIM, (h + j + 1) * HEAD_DIM)
                att_ref[rows[half], out] = att[:, own].T.astype(jnp.bfloat16)
                dq_ref[rows[half], out] = grad[:, own].T.astype(jnp.bfloat16)

    for half in (0, 1):
        key_own = matmul(d_buf[half, :st], gather(q_buf, half, 0, heads)) * scaling
        value_own = matmul(p_buf[half, :st], gather(g_buf, half, 0, heads))
        for d in range(1, reach + 1):
            arrives = me >= d
            if half == 0:
                joined = (me + d < n) & (last - 2 * me - d <= reach)
                arrives = jnp.logical_not(joined) & (last - me - d != me)

            @pl.when(arrives)
            def _():
                part_copy(half, d, me, half).wait_recv()

        for d in range(reach):
            key_own += part_in[half, d, :st].astype(jnp.float32)
            value_own += part_in[half, d, st:].astype(jnp.float32)
        dk_ref[rows[half]] = key_own.astype(jnp.bfloat16)
        dv_ref[rows[half]] = value_own.astype(jnp.bfloat16)

    for half in (0, 1):
        kv_routes(half, lambda copy: copy.wait_send())
        part_routes(half, lambda copy: copy.wait_send())


def write_out(*refs):
    sems = refs[8]
    copies = [pltpu.make_async_copy(refs[i], refs[4 + i], sems.at[i]) for i in range(4)]
    for copy in copies:
        copy.start()
    for copy in copies:
        copy.wait()


def shards(query_rows, key_rows, value_rows, out_grad, doc_lengths):
    n = lax.axis_size("ctx")
    reach = min(DOC_STRETCHES, n // 4)
    tok, width = query_rows.shape
    st = tok // 2
    heads = width // HEAD_DIM
    low = jnp.bfloat16
    vmem = pl.BlockSpec(memory_space=pltpu.VMEM)
    hbm = pl.BlockSpec(memory_space=pltpu.HBM)
    anywhere = pl.BlockSpec(memory_space=pl.ANY)
    like = lambda x: jax.ShapeDtypeStruct(x.shape, low)
    macs = 2 * heads * st * st * (reach + 1) * HEAD_DIM * 6
    shapes = (like(query_rows), like(query_rows), like(key_rows), like(key_rows))
    results = pl.pallas_call(
        functools.partial(kernel, n, reach, heads),
        out_shape=shapes,
        in_specs=[hbm, hbm, hbm, hbm, hbm],
        out_specs=(vmem,) * 4,
        scratch_shapes=[
            pltpu.SMEM(doc_lengths.shape, jnp.int32),
            pltpu.VMEM((2, st, width), low),
            pltpu.VMEM((2, st, width), low),
            pltpu.VMEM((2, reach + 1, st, HEAD_DIM), low),
            pltpu.VMEM((2, reach + 1, st, HEAD_DIM), low),
            pltpu.VMEM((2, st, width), jnp.float32),
            pltpu.VMEM((2, st, width), jnp.float32),
            pltpu.VMEM((2, (reach + 1) * st, width), low),
            pltpu.VMEM((2, (reach + 1) * st, width), low),
            pltpu.VMEM((2, reach, 2 * st, HEAD_DIM), low),
            pltpu.VMEM((2, reach, 2 * st, HEAD_DIM), low),
            pltpu.SemaphoreType.DMA,
            pltpu.SemaphoreType.DMA((2, 4)),
            pltpu.SemaphoreType.DMA((2, reach, 2)),
            pltpu.SemaphoreType.DMA((2, reach, 2)),
            pltpu.SemaphoreType.DMA((2, reach)),
            pltpu.SemaphoreType.DMA((2, reach)),
        ],
        compiler_params=pltpu.CompilerParams(
            collective_id=0, has_side_effects=True, vmem_limit_bytes=40 * 1024 * 1024
        ),
        cost_estimate=pl.CostEstimate(
            flops=2 * macs,
            bytes_accessed=8 * tok * width + 8 * tok * HEAD_DIM,
            transcendentals=2 * heads * st * st * reach,
        ),
    )(*[
        pltpu.with_memory_space_constraint(x, pltpu.HBM)
        for x in (doc_lengths, query_rows, key_rows, value_rows, out_grad)
    ])
    return pl.pallas_call(
        write_out,
        out_shape=shapes,
        in_specs=[anywhere] * 4,
        out_specs=(hbm,) * 4,
        scratch_shapes=[pltpu.SemaphoreType.DMA((4,))],
        compiler_params=pltpu.CompilerParams(vmem_limit_bytes=4 * 1024 * 1024),
    )(*results)


def solution(mesh):
    rows = P(("groups", "ctx"), "head")
    return jax.shard_map(
        shards,
        mesh=mesh,
        in_specs=(rows, rows, rows, rows, P("groups")),
        out_specs=(rows,) * 4,
        check_vma=False,
    )
```

```python
import functools
import math

import jax
import jax.numpy as jnp
from jax import lax
from jax.experimental import pallas as pl
from jax.experimental.pallas import tpu as pltpu
from jax.sharding import PartitionSpec as P

HEAD_DIM = 128
DOC_STRETCHES = 8
PAIR = 2
MESH = pl.DeviceIdType.MESH


def kernel(
    n,
    reach,
    heads,
    docs_hbm,
    q_hbm,
    k_hbm,
    v_hbm,
    g_hbm,
    att_ref,
    dq_ref,
    dk_ref,
    dv_ref,
    docs_ref,
    q_buf,
    g_buf,
    q_turn,
    g_turn,
    k_buf,
    v_buf,
    s_own,
    w_own,
    p_buf,
    d_buf,
    part_out,
    part_in,
    docs_sem,
    load_sem,
    kv_send,
    kv_recv,
    part_send,
    part_recv,
):
    st = q_hbm.shape[0] // 2
    me = lax.axis_index("ctx")
    last = 2 * n - 1
    scaling = HEAD_DIM**-0.5
    wide = PAIR * HEAD_DIM
    rows = [slice(half * st, (half + 1) * st) for half in range(2)]
    dot = functools.partial(lax.dot_general, preferred_element_type=jnp.float32)

    def matmul(a, b):
        return dot(a, b, (((1,), (0,)), ((), ())))

    barrier = pltpu.get_barrier_semaphore()
    for by in range(1, reach + 1):
        for sign in (-1, 1):
            other = me + sign * by

            @pl.when((other >= 0) & (other < n))
            def _():
                pl.semaphore_signal(
                    barrier, inc=1, device_id={"ctx": other}, device_id_type=MESH
                )

    docs_copy = pltpu.make_async_copy(docs_hbm, docs_ref, docs_sem)
    docs_copy.start()
    loads = []
    for half in range(2):
        for slot, (src, dst) in enumerate(
            (
                (k_hbm, k_buf.at[half, 0]),
                (q_hbm, q_buf.at[half]),
                (v_hbm, v_buf.at[half, 0]),
                (g_hbm, g_buf.at[half]),
            )
        ):
            copy = pltpu.make_async_copy(src.at[rows[half]], dst, load_sem.at[half, slot])
            copy.start()
            loads.append(copy)

    for d in range(1, reach + 1):

        @pl.when(me < d)
        def _():
            k_buf[0, d] = jnp.zeros_like(k_buf[0, d])
            v_buf[0, d] = jnp.zeros_like(v_buf[0, d])
            part_in[1, d - 1] = jnp.zeros_like(part_in[1, d - 1])

        @pl.when((me + d < n) & (last - 2 * me - d <= reach))
        def _():
            part_in[0, d - 1] = jnp.zeros_like(part_in[0, d - 1])

    pl.semaphore_wait(barrier, jnp.minimum(me, reach) + jnp.minimum(n - 1 - me, reach))

    def kv_copy(which, half, d, target, to_half):
        src, dst = ((k_hbm, k_buf), (v_hbm, v_buf))[which]
        return pltpu.make_async_remote_copy(
            src_ref=src.at[rows[half]],
            dst_ref=dst.at[to_half, d],
            send_sem=kv_send.at[half, d - 1, which],
            recv_sem=kv_recv.at[to_half, d - 1, which],
            device_id={"ctx": target},
            device_id_type=MESH,
        )

    def kv_routes(act):
        for d in range(1, reach + 1):
            up = me + d
            fold = last - up

            @pl.when(up < n)
            def _():
                for which in range(2):
                    act(kv_copy(which, 0, d, up, 0))

            @pl.when((up >= n) & (fold < me))
            def _():
                for which in range(2):
                    act(kv_copy(which, 0, d, fold, 1))

            @pl.when(me >= d)
            def _():
                for which in range(2):
                    act(kv_copy(which, 1, d, me - d, 1))

    def kv_arrive(half):
        for d in range(1, reach + 1):
            source = last - me - d
            for which in range(2):
                arrives = (me >= d) if half == 0 else (source > me)

                @pl.when(arrives)
                def _():
                    kv_copy(which, half, d, me, half).wait_recv()

    kv_routes(lambda copy: copy.start())

    docs_copy.wait()

    lane = lax.broadcasted_iota(jnp.int32, (st, st), 1)
    sub = lax.broadcasted_iota(jnp.int32, (st, st), 0)
    lower = sub <= lane
    lower_low = lower.astype(jnp.float32).astype(jnp.bfloat16)
    lower_wide = jnp.concatenate([lower] * PAIR, axis=1)
    lower_low = jnp.concatenate([lower_low] * PAIR, axis=1)
    bias = []
    for half in range(2):
        stretch = me if half == 0 else last - me
        base = stretch * st
        row_pos = base + lane[:8]
        first = jnp.zeros((8, st), jnp.int32)
        begin = jnp.int32(0)
        for i in range(docs_ref.shape[0]):
            first = jnp.where(row_pos >= begin, begin, first)
            begin = begin + docs_ref[i]
        first = first[:1] - base
        blocks = [jnp.where(lower, sub, sub - reach * st)]
        blocks += [sub - d * st for d in range(1, reach)]
        blocks = [jnp.where(block >= first, 0.0, -1e30) for block in blocks]
        bias.append([jnp.concatenate([block] * PAIR, axis=1) for block in blocks])

    def gather(buf, half, first, count):
        cols = [
            buf[half, :, h * HEAD_DIM : (h + 1) * HEAD_DIM] for h in range(first, first + count)
        ]
        return jnp.concatenate(cols, axis=0)

    for copy in loads:
        copy.wait()

    for half in (0, 1):
        for h in range(0, heads, PAIR):
            cols = slice(h * HEAD_DIM, h * HEAD_DIM + wide)
            for j in range(h, h + PAIR):
                own = slice(j * HEAD_DIM, (j + 1) * HEAD_DIM)
                q_turn[half, :, own] = q_buf[half, :, own].T
                g_turn[half, :, own] = g_buf[half, :, own].T
            s_own[half, :, cols] = matmul(k_buf[half, 0], q_turn[half, :, cols])
            w_own[half, :, cols] = matmul(v_buf[half, 0], g_turn[half, :, cols])

    def part_copy(half, d, target, to_half):
        return pltpu.make_async_remote_copy(
            src_ref=part_out.at[half, d - 1],
            dst_ref=part_in.at[to_half, d - 1],
            send_sem=part_send.at[half, d - 1],
            recv_sem=part_recv.at[to_half, d - 1],
            device_id={"ctx": target},
            device_id_type=MESH,
        )

    def part_routes(half, act):
        for d in range(1, reach + 1):
            up = me + d
            fold = last - up
            if half == 0:

                @pl.when((me >= d) & (last - 2 * me + d > reach))
                def _():
                    act(part_copy(0, d, me - d, 0))

            else:

                @pl.when(up < n)
                def _():
                    act(part_copy(1, d, up, 1))

                @pl.when((up >= n) & (fold != me))
                def _():
                    act(part_copy(1, d, fold, 0))

    def give_back(half):
        if half == 1:
            for d in range(1, reach + 1):
                fold = last - me - d

                @pl.when(fold < me)
                def _():
                    both = part_out[1, d - 1].astype(jnp.float32)
                    both += part_out[0, me - fold - 1].astype(jnp.float32)
                    part_out[1, d - 1] = both.astype(jnp.bfloat16)

                @pl.when(fold == me)
                def _():
                    part_in[0, d - 1] = part_out[1, d - 1]

        part_routes(half, lambda copy: copy.start())

    factor = scaling * math.log2(math.e)
    for half in (0, 1):
        kv_arrive(half)
        if half == 1:
            for d in range(1, reach + 1):
                source = last - me - d

                @pl.when(source <= me)
                def _():
                    k_buf[1, d] = k_buf[0, me - source]
                    v_buf[1, d] = v_buf[0, me - source]

        k_rest = k_buf[half, 1:].reshape(reach * st, HEAD_DIM)
        v_rest = v_buf[half, 1:].reshape(reach * st, HEAD_DIM)
        for h in range(0, heads, PAIR):
            cols = slice(h * HEAD_DIM, h * HEAD_DIM + wide)

            def blocks(own, rest):
                merged = jnp.where(lower_wide, own[half, :, cols], rest[(reach - 1) * st :])
                return [merged] + [rest[(d - 1) * st : d * st] for d in range(1, reach)]

            scores = blocks(s_own, matmul(k_rest, q_turn[half, :, cols]))
            scores = [score + mask for score, mask in zip(scores, bias[half])]
            top = functools.reduce(jnp.maximum, scores)
            top = jnp.max(top, axis=0, keepdims=True)
            weights = [jnp.exp2((score - top) * factor) for score in scores]
            total = jnp.sum(functools.reduce(jnp.add, weights), axis=0, keepdims=True)
            inverse = 1.0 / total
            weights = [weight * inverse for weight in weights]
            grads = blocks(w_own, matmul(v_rest, g_turn[half, :, cols]))
            delta = functools.reduce(jnp.add, [w * g for w, g in zip(weights, grads)])
            delta = jnp.sum(delta, axis=0, keepdims=True)
            for d in range(reach):
                low = weights[d].astype(jnp.bfloat16)
                slope = (weights[d] * (grads[d] - delta)).astype(jnp.bfloat16)
                if d == 0:
                    low_own = low * lower_low
                    slope_own = slope * lower_low
                    p_buf[half, :st, cols] = low_own
                    d_buf[half, :st, cols] = slope_own
                    p_buf[half, reach * st :, cols] = low - low_own
                    d_buf[half, reach * st :, cols] = slope - slope_own
                else:
                    p_buf[half, d * st : (d + 1) * st, cols] = low
                    d_buf[half, d * st : (d + 1) * st, cols] = slope

        part_out[half, :, :st] = (
            (matmul(d_buf[half, st:], gather(q_buf, half, 0, heads)) * scaling)
            .astype(jnp.bfloat16)
            .reshape(reach, st, HEAD_DIM)
        )
        part_out[half, :, st:] = (
            matmul(p_buf[half, st:], gather(g_buf, half, 0, heads))
            .astype(jnp.bfloat16)
            .reshape(reach, st, HEAD_DIM)
        )
        give_back(half)

    for half in (0, 1):
        k_turn = jnp.concatenate([k_buf[half, d].T for d in range(reach + 1)], axis=1)
        v_turn = jnp.concatenate([v_buf[half, d].T for d in range(reach + 1)], axis=1)
        for h in range(0, heads, PAIR):
            cols = slice(h * HEAD_DIM, h * HEAD_DIM + wide)
            att = matmul(v_turn, p_buf[half, :, cols])
            grad = matmul(k_turn, d_buf[half, :, cols]) * scaling
            for j in range(PAIR):
                own = slice(j * HEAD_DIM, (j + 1) * HEAD_DIM)
                out = slice((h + j) * HEAD_DIM, (h + j + 1) * HEAD_DIM)
                att_ref[rows[half], out] = att[:, own].T.astype(jnp.bfloat16)
                dq_ref[rows[half], out] = grad[:, own].T.astype(jnp.bfloat16)

    for half in (0, 1):
        key_own = matmul(d_buf[half, :st], gather(q_buf, half, 0, heads)) * scaling
        value_own = matmul(p_buf[half, :st], gather(g_buf, half, 0, heads))
        for d in range(1, reach + 1):
            arrives = me >= d
            if half == 0:
                joined = (me + d < n) & (last - 2 * me - d <= reach)
                arrives = jnp.logical_not(joined) & (last - me - d != me)

            @pl.when(arrives)
            def _():
                part_copy(half, d, me, half).wait_recv()

        for d in range(reach):
            key_own += part_in[half, d, :st].astype(jnp.float32)
            value_own += part_in[half, d, st:].astype(jnp.float32)
        dk_ref[rows[half]] = key_own.astype(jnp.bfloat16)
        dv_ref[rows[half]] = value_own.astype(jnp.bfloat16)

    kv_routes(lambda copy: copy.wait_send())
    for half in (0, 1):
        part_routes(half, lambda copy: copy.wait_send())


def write_out(*refs):
    sems = refs[8]
    copies = [pltpu.make_async_copy(refs[i], refs[4 + i], sems.at[i]) for i in range(4)]
    for copy in copies:
        copy.start()
    for copy in copies:
        copy.wait()


def shards(query_rows, key_rows, value_rows, out_grad, doc_lengths):
    n = lax.axis_size("ctx")
    reach = min(DOC_STRETCHES, n // 4)
    tok, width = query_rows.shape
    st = tok // 2
    heads = width // HEAD_DIM
    low = jnp.bfloat16
    vmem = pl.BlockSpec(memory_space=pltpu.VMEM)
    hbm = pl.BlockSpec(memory_space=pltpu.HBM)
    anywhere = pl.BlockSpec(memory_space=pl.ANY)
    like = lambda x: jax.ShapeDtypeStruct(x.shape, low)
    macs = 2 * heads * st * st * (reach + 1) * HEAD_DIM * 6
    shapes = (like(query_rows), like(query_rows), like(key_rows), like(key_rows))
    results = pl.pallas_call(
        functools.partial(kernel, n, reach, heads),
        out_shape=shapes,
        in_specs=[hbm, hbm, hbm, hbm, hbm],
        out_specs=(vmem,) * 4,
        scratch_shapes=[
            pltpu.SMEM(doc_lengths.shape, jnp.int32),
            pltpu.VMEM((2, st, width), low),
            pltpu.VMEM((2, st, width), low),
            pltpu.VMEM((2, HEAD_DIM, width), low),
            pltpu.VMEM((2, HEAD_DIM, width), low),
            pltpu.VMEM((2, reach + 1, st, HEAD_DIM), low),
            pltpu.VMEM((2, reach + 1, st, HEAD_DIM), low),
            pltpu.VMEM((2, st, width), jnp.float32),
            pltpu.VMEM((2, st, width), jnp.float32),
            pltpu.VMEM((2, (reach + 1) * st, width), low),
            pltpu.VMEM((2, (reach + 1) * st, width), low),
            pltpu.VMEM((2, reach, 2 * st, HEAD_DIM), low),
            pltpu.VMEM((2, reach, 2 * st, HEAD_DIM), low),
            pltpu.SemaphoreType.DMA,
            pltpu.SemaphoreType.DMA((2, 4)),
            pltpu.SemaphoreType.DMA((2, reach, 2)),
            pltpu.SemaphoreType.DMA((2, reach, 2)),
            pltpu.SemaphoreType.DMA((2, reach)),
            pltpu.SemaphoreType.DMA((2, reach)),
        ],
        compiler_params=pltpu.CompilerParams(
            collective_id=0, has_side_effects=True, vmem_limit_bytes=40 * 1024 * 1024
        ),
        cost_estimate=pl.CostEstimate(
            flops=2 * macs,
            bytes_accessed=8 * tok * width + 8 * tok * HEAD_DIM,
            transcendentals=2 * heads * st * st * reach,
        ),
    )(*[
        pltpu.with_memory_space_constraint(x, pltpu.HBM)
        for x in (doc_lengths, query_rows, key_rows, value_rows, out_grad)
    ])
    return pl.pallas_call(
        write_out,
        out_shape=shapes,
        in_specs=[anywhere] * 4,
        out_specs=(hbm,) * 4,
        scratch_shapes=[pltpu.SemaphoreType.DMA((4,))],
        compiler_params=pltpu.CompilerParams(vmem_limit_bytes=4 * 1024 * 1024),
    )(*results)


def solution(mesh):
    rows = P(("groups", "ctx"), "head")
    return jax.shard_map(
        shards,
        mesh=mesh,
        in_specs=(rows, rows, rows, rows, P("groups")),
        out_specs=(rows,) * 4,
        check_vma=False,
    )
```
